512 devices in a mesh: dom: 128 (over y, z, core), rep: 4 (over x).
Axes of the slice: x: 4, y: 4, z: 16, core: 2. Of those that a mesh axis runs over, the one named last changes fastest.
Arguments:
- entity: bfloat16 [128, 512, 400], P(None, 'dom'), may hold values from -4 to 4
- relation: bfloat16 [2000, 400], replicated, may hold values from -3 to 3
- head_ids: int32 [512000], P(('dom', 'rep')), may hold values from 0 to 511
- relation_ids: int32 [512000], P(('dom', 'rep')), may hold values from 0 to 1999
- tail_ids: int32 [512000], P(('dom', 'rep')), may hold values from 0 to 511
- negative_ids: int32 [512, 1000], P(('dom', 'rep')), may hold values from 0 to 511
- span_counts: int32 [512], P(('dom', 'rep')), may hold values from 1 to 1000, 358400 in all
- plan: int32 [128, 2], replicated, may hold values from 0 to 127
Outputs:
- entity_grad: bfloat16 [128, 512, 400], P(None, ('dom', 'rep'))
- relation_grad: bfloat16 [2000, 400], replicated
The draws below stay inside these ranges and needn't reach their ends.
Inputs may be any that keep to these rules, and one draw needn't show every extreme that they name: `span_counts`: some span is full. `plan`: uneven: a partition may serve several buckets or none.
All inputs are finite; a program needn't handle non-finite values. No bound on the sum of `span_counts` on one device may be relied on, other than what follows from the above.
Results may differ from the reference program's by a relative error of at most 0.014.
Values may be sent and summed in bfloat16 or wider, within the bound.
A program may use at most 64 MiB of HBM per device.

```python
import math
import jax
import jax.numpy as jnp
import numpy as np
from jax import lax

D = 400
RELS = 2000
SPAN = 1000
NEG = 1000
PS = 4
PART_ROWS = 512
SPANS = 512
EDGES = 512000
N_DOM = 128
N_REP = 4


def draw_entity(key, part):
    key = jax.random.fold_in(key, 11)
    key_entries, key_scales = jax.random.split(key, 2)
    array_shape = (N_DOM, PS * N_DOM, D)
    entries = jnp.clip(jax.random.normal(key_entries, array_shape, jnp.float32), -4.0, 4.0) * 0.5
    row_scale = jnp.exp(jax.random.uniform(key_scales, (N_DOM, PS * N_DOM, 1), jnp.float32, jnp.log(0.5), jnp.log(2.0)))
    return (entries * row_scale).astype(jnp.bfloat16)


def draw_relation(key, part):
    key = jax.random.fold_in(key, 13)
    key_real = jax.random.fold_in(key, 0)
    return jnp.clip(jax.random.normal(key_real, (RELS, D), jnp.float32) * 0.5, -3.0, 3.0).astype(jnp.bfloat16)


def with_ends(result, stream_key, smallest, high):
    extent = result.shape
    place = [jax.random.randint(jax.random.fold_in(stream_key, axis), (), 0, extent[axis]) for axis in range(len(extent))]
    result = result.at[tuple(place)].set(smallest)
    longest = extent.index(max(extent))
    place[longest] = (place[longest] + 1) % extent[longest]
    return result.at[tuple(place)].set(high)


def cumulative_ranks(count, lean):
    loads = [(1 << 20) // math.isqrt(rank ** lean) + 1 for rank in range(1, count + 1)]
    width = 1 + sum(loads) // (1 << 30)
    return np.cumsum(np.array([max(1, weight // width) for weight in loads]))


def skewed_ids(own_key, extent, amount, slope):
    table = cumulative_ranks(amount, slope)
    lot = jax.random.randint(jax.random.fold_in(own_key, 1), extent, 0, int(table[amount - 1]))
    grade = jnp.searchsorted(jnp.asarray(table, jnp.int32), lot, side="right")
    return jax.random.permutation(jax.random.fold_in(own_key, 2), amount)[grade].astype(jnp.int32)


def profile(number_of, total, most, skew):
    weights = [(1 << 20) // math.isqrt(grade ** skew) + 1 for grade in range(2, number_of + 1)]
    rest, given = total - most - (number_of - 1), [1] * (number_of - 1)
    while rest > 0:
        movable = [i for i in range(number_of - 1) if given[i] < most]
        pool, left = sum([weights[i] for i in movable]), rest
        for i in movable:
            extra = min(most - given[i], max(1, left * weights[i] // pool), rest)
            given[i] = given[i] + extra
            rest = rest - extra
    return np.array([most] + given)


def ragged_sizes(own_key, number_of, total, reach, lean):
    if number_of == 2:
        one = jax.random.randint(own_key, (), max(1, total - reach), min(reach, total - 1) + 1)
        return jnp.stack([one, total - one])
    tallies = jnp.asarray(profile(number_of, total, reach, lean), jnp.int32)
    couples = (number_of - 1) // 2
    donor, sink = tallies[1:1 + 2 * couples:2], tallies[2:2 + 2 * couples:2]
    margin = jnp.minimum(donor - 1, reach - sink)
    moved = jax.random.randint(jax.random.fold_in(own_key, 1), (couples,), 0, 1 << 20) % (margin + 1)
    tallies = tallies.at[1:1 + 2 * couples:2].set(donor - moved).at[2:2 + 2 * couples:2].set(sink + moved)
    return tallies[jax.random.permutation(jax.random.fold_in(own_key, 2), number_of)]


def setup_inputs(seed: int = 0) -> dict:
    keys = jax.random.split(jax.random.key(seed), 9)
    return {
        "entity": draw_entity(jax.random.fold_in(keys[8], 71), 0),
        "relation": draw_relation(jax.random.fold_in(keys[8], 71), 0),
        "head_ids": with_ends(jax.random.randint(keys[2], (EDGES,), 0, PART_ROWS), jax.random.fold_in(keys[2], 1), 0, PART_ROWS - 1).astype(jnp.int32),
        "relation_ids": with_ends(jax.random.randint(keys[3], (EDGES,), 0, RELS), jax.random.fold_in(keys[3], 1), 0, RELS - 1).astype(jnp.int32),
        "tail_ids": with_ends(jax.random.randint(keys[4], (EDGES,), 0, PART_ROWS), jax.random.fold_in(keys[4], 1), 0, PART_ROWS - 1).astype(jnp.int32),
        "negative_ids": with_ends(jax.random.randint(keys[5], (SPANS, NEG), 0, PART_ROWS), jax.random.fold_in(keys[5], 1), 0, PART_ROWS - 1).astype(jnp.int32),
        "span_counts": ragged_sizes(keys[6], SPANS, 7 * SPAN * N_DOM * N_REP // 10, SPAN, 2).astype(jnp.int32),
        "plan": with_ends(skewed_ids(keys[7], (N_DOM, 2), N_DOM, 2), jax.random.fold_in(keys[7], 3), 0, N_DOM - 1).astype(jnp.int32),
    }


def edge_grads(head_rows, relation_rows, tail_rows, noise_rows, valid_mask):
    half_width = head_rows.shape[1] // 2
    head_full = head_rows.astype(jnp.float32)
    relation_full = relation_rows.astype(jnp.float32)
    tail_full = tail_rows.astype(jnp.float32)
    head_real, head_imag = head_full[:, :half_width], head_full[:, half_width:]
    relation_real, relation_imag = relation_full[:, :half_width], relation_full[:, half_width:]
    queries = jnp.concatenate([head_real * relation_real - head_imag * relation_imag,
                               head_real * relation_imag + head_imag * relation_real], axis=1)
    queries_low = queries.astype(jnp.bfloat16)
    positive = jnp.sum(queries * tail_full, axis=1)
    negative = lax.dot_general(queries_low, noise_rows, (((1,), (1,)), ((), ())),
                               preferred_element_type=jnp.float32)
    peak_score = jnp.maximum(jnp.max(negative, axis=1), positive)
    positive_exp = jnp.exp(positive - peak_score)
    negative_exp = jnp.exp(negative - peak_score[:, None])
    denominator = positive_exp + jnp.sum(negative_exp, axis=1)
    positive_grad = valid_mask * (positive_exp / denominator - 1.0)
    negative_grad = (negative_exp * (valid_mask / denominator)[:, None]).astype(jnp.bfloat16)
    queries_grad = positive_grad[:, None] * tail_full + jnp.dot(negative_grad, noise_rows,
                                                                preferred_element_type=jnp.float32)
    tail_grad = positive_grad[:, None] * queries
    noise_grad = lax.dot_general(negative_grad, queries_low, (((0,), (0,)), ((), ())),
                                 preferred_element_type=jnp.float32)
    grad_real, grad_imag = queries_grad[:, :half_width], queries_grad[:, half_width:]
    head_grad = jnp.concatenate([grad_real * relation_real + grad_imag * relation_imag,
                                 -grad_real * relation_imag + grad_imag * relation_real], axis=1)
    relation_grad = jnp.concatenate([grad_real * head_real + grad_imag * head_imag,
                                     -grad_real * head_imag + grad_imag * head_real], axis=1)
    return head_grad, relation_grad, tail_grad, noise_grad


def reference(entity, relation, head_ids, relation_ids, tail_ids, negative_ids, span_counts, plan):
    part_count, row_count, full_width = entity.shape
    rel_count = relation.shape[0]

    def one_span(state_pair, device_index):
        entity_sum, relation_sum = state_pair
        worker = device_index // N_REP
        head_part = plan[worker, 0]
        tail_part = plan[worker, 1]
        head_block = entity[head_part]
        tail_block = entity[tail_part]
        slot_start = (device_index * SPAN).astype(jnp.int32)
        head_local = lax.dynamic_slice_in_dim(head_ids, slot_start, SPAN)
        relation_local = lax.dynamic_slice_in_dim(relation_ids, slot_start, SPAN)
        tail_local = lax.dynamic_slice_in_dim(tail_ids, slot_start, SPAN)
        noise_local = negative_ids[device_index]
        valid_mask = (jnp.arange(SPAN, dtype=jnp.int32) < span_counts[device_index]).astype(jnp.float32)
        head_grad, relation_grad, tail_grad, noise_grad = edge_grads(
            head_block[head_local], relation[relation_local], tail_block[tail_local],
            tail_block[noise_local], valid_mask)
        head_sum = jax.ops.segment_sum(head_grad, head_local, num_segments=row_count)
        tail_sum = (jax.ops.segment_sum(tail_grad, tail_local, num_segments=row_count)
                    + jax.ops.segment_sum(noise_grad, noise_local, num_segments=row_count))
        entity_sum = entity_sum.at[head_part].add(head_sum)
        entity_sum = entity_sum.at[tail_part].add(tail_sum)
        relation_sum = relation_sum + jax.ops.segment_sum(relation_grad, relation_local, num_segments=rel_count)
        return (entity_sum, relation_sum), None

    start_state = (jnp.zeros((part_count, row_count, full_width), jnp.float32),
                   jnp.zeros((rel_count, full_width), jnp.float32))
    (entity_sum, relation_sum), _ = lax.scan(one_span, start_state,
                                             jnp.arange(N_DOM * N_REP, dtype=jnp.int32))
    return (entity_sum.astype(jnp.bfloat16), relation_sum.astype(jnp.bfloat16))
```

```python
import functools

import jax
import jax.numpy as jnp
from jax import lax
from jax.experimental import pallas as pl
from jax.experimental.pallas import tpu as pltpu
from jax.sharding import PartitionSpec as P

MESH = pl.DeviceIdType.MESH
F32, BF16, I32 = jnp.float32, jnp.bfloat16, jnp.int32
VMEM = pl.BlockSpec(memory_space=pltpu.VMEM)
SMEM = pl.BlockSpec(memory_space=pltpu.SMEM)

NY, NZ, NC, NX = 4, 16, 2, 4
NYC = NY * NC
NDOM = NY * NZ * NC
D = 400
HALF = D // 2
RELS = 2000
SPAN = 1000
SLOTS = 1024
CHUNK = 256
ROWS = 512
QUART = 256
YROWS = 112
YPAD = 128
NEVER = -1e30


def nn(a, b):
    return lax.dot_general(a, b, (((1,), (0,)), ((), ())), preferred_element_type=F32)


def nt(a, b):
    return lax.dot_general(a, b, (((1,), (1,)), ((), ())), preferred_element_type=F32)


def tn(a, b):
    return lax.dot_general(a, b, (((0,), (0,)), ((), ())), preferred_element_type=F32)


def iota(shape, axis):
    return lax.broadcasted_iota(I32, shape, axis)


def onehot(hit):
    return jnp.where(hit, 1.0, 0.0).astype(BF16)


class Place:
    def __init__(self):
        dom, self.x = lax.axis_index("dom"), lax.axis_index("rep")
        self.c = lax.rem(dom, NC)
        self.z = lax.rem(lax.div(dom, NC), NZ)
        self.y = lax.div(dom, NC * NZ)
        self.yc = self.y * NC + self.c
        self.dom = dom

    def at(self, z=None, yc=None, x=None):
        z = self.z if z is None else z
        yc = self.yc if yc is None else yc
        x = self.x if x is None else x
        return {"dom": (lax.div(yc, NC) * NZ + z) * NC + lax.rem(yc, NC), "rep": x}

    def others(self, axis, body):
        size, me = {"z": (NZ, self.z), "yc": (NYC, self.yc), "x": (NX, self.x), "y": (NY, self.y)}[axis]

        def step(k, carry):
            body(lax.rem(me + k, size))
            return carry

        lax.fori_loop(1, size, step, 0)

    def barrier(self):
        sem = pltpu.get_barrier_semaphore()

        def hello(**where):
            pl.semaphore_signal(sem, inc=1, device_id=self.at(**where), device_id_type=MESH)

        self.others("x", lambda p: hello(x=p))
        self.others("yc", lambda p: hello(yc=p))
        self.others("z", lambda p: hello(z=p))
        pl.semaphore_wait(sem, NX + NYC + NZ - 3)


def remote(src, dst, send, recv, where):
    return pltpu.make_async_remote_copy(
        src_ref=src, dst_ref=dst, send_sem=send, recv_sem=recv, device_id=where, device_id_type=MESH
    )


def worker_major(shape, row_axis):
    row, col = iota(shape, row_axis), iota(shape, 1 - row_axis)
    half = lax.bitwise_and(row, 1)
    core = lax.bitwise_and(lax.shift_right_logical(row, 1), 1)
    y = lax.bitwise_and(lax.shift_right_logical(row, 2), 3)
    z = lax.shift_right_logical(row, 4)
    return onehot(col == half * NDOM + (y * NZ + z) * NC + core)


def swap_zy(shape, row_axis):
    row, col = iota(shape, row_axis), iota(shape, 1 - row_axis)
    half = lax.bitwise_and(row, 1)
    z = lax.bitwise_and(lax.shift_right_logical(row, 1), 15)
    yc = lax.shift_right_logical(row, 5)
    return onehot(col == z * 16 + yc * 2 + half)


def gather_kernel(ent, plan, out, snd1, rcv1, snd2, rcv2, s1, r1, s2, r2, s3, r3):
    me = Place()
    me.barrier()
    stripe = ent[me.x]
    sq = (NDOM, NDOM)
    picked = [nn(stripe, onehot(iota(sq, 0) == plan[h : h + 1, :])).astype(BF16) for h in range(2)]
    wide = jnp.concatenate(picked, axis=1)
    mat = (2 * NDOM, 2 * NDOM)
    snd1[...] = nt(worker_major(mat, 0), wide).astype(BF16).reshape(snd1.shape)

    def copy1(dst, src):
        return remote(snd1.at[dst], rcv1.at[src], s1.at[dst], r1.at[src], me.at(z=dst))

    me.others("z", lambda p: copy1(p, me.z).start())
    rcv1[me.z] = snd1[me.z]
    me.others("z", lambda p: copy1(p, p).wait_recv())
    snd2[...] = nn(swap_zy(mat, 0), rcv1[...].reshape(2 * NDOM, D)).astype(BF16).reshape(snd2.shape)

    def copy2(dst, src):
        return remote(snd2.at[dst], rcv2.at[src], s2.at[dst], r2.at[src], me.at(yc=dst))

    me.others("yc", lambda p: copy2(p, me.yc).start())
    rcv2[me.yc] = snd2[me.yc]
    me.others("yc", lambda p: copy2(p, p).wait_recv())
    row, col = iota(mat, 0), iota(mat, 1)
    half = lax.bitwise_and(row, 1)
    z = lax.bitwise_and(lax.shift_right_logical(row, 1), 15)
    yc = lax.shift_right_logical(row, 5)
    owner = (lax.shift_right_logical(yc, 1) * NZ + z) * NC + lax.bitwise_and(yc, 1)
    back = onehot(col == half * NDOM + owner)
    out[me.x] = tn(rcv2[...].reshape(2 * NDOM, D), back).astype(BF16)

    def copy3(dst, src):
        return remote(out.at[src], out.at[src], s3.at[dst], r3.at[src], me.at(x=dst))

    me.others("x", lambda p: copy3(p, me.x).start())
    me.others("x", lambda p: copy3(p, p).wait_recv())
    me.others("z", lambda p: copy1(p, me.z).wait_send())
    me.others("yc", lambda p: copy2(p, me.yc).wait_send())
    me.others("x", lambda p: copy3(p, me.x).wait_send())


def gather(ent, plan):
    dma = pltpu.SemaphoreType.DMA
    return pl.pallas_call(
        gather_kernel,
        out_shape=jax.ShapeDtypeStruct((NX, D, 2 * NDOM), BF16),
        in_specs=[VMEM, VMEM],
        out_specs=VMEM,
        scratch_shapes=[
            pltpu.VMEM((NZ, 2 * NYC, D), BF16),
            pltpu.VMEM((NZ, 2 * NYC, D), BF16),
            pltpu.VMEM((NYC, 2 * NZ, D), BF16),
            pltpu.VMEM((NYC, 2 * NZ, D), BF16),
            dma((NZ,)),
            dma((NZ,)),
            dma((NYC,)),
            dma((NYC,)),
            dma((NX,)),
            dma((NX,)),
        ],
        compiler_params=pltpu.CompilerParams(
            collective_id=0, has_side_effects=True, vmem_limit_bytes=40 << 20
        ),
        name="gather_rows",
    )(ent, plan)


def span_kernel(
    got, rel, head, relid, tail, neg, count, rel_sum, ent_sum, ids, hb, tb, tr, logc, h1, r1, dr, dh, av, ql
):
    ids[...] = jnp.full(ids.shape, -4, I32)
    for k, ref in enumerate((head, relid, tail, neg)):
        ids[k : k + 1, 0:SPAN] = ref[...]
    raw = ids[...]
    place = lax.bitwise_and(raw, 3) * NDOM + lax.shift_right_arithmetic(raw, 2)
    ids[...] = jnp.where(iota(ids.shape, 0) == 1, raw, place)
    for x in range(NX):
        hb[:, x * NDOM : (x + 1) * NDOM] = got[x, :, 0:NDOM]
        tb[:, x * NDOM : (x + 1) * NDOM] = got[x, :, NDOM:]
    tr[...] = tb[...].T
    times = jnp.zeros((ROWS, 1), F32)
    for k in range(SLOTS // CHUNK):
        hit = iota((ROWS, CHUNK), 0) == ids[3:4, k * CHUNK : (k + 1) * CHUNK]
        times += jnp.sum(jnp.where(hit, 1.0, 0.0), axis=1, keepdims=True)
    logc[...] = jnp.where(times > 0.0, jnp.log(jnp.maximum(times, 1.0)), NEVER)

    def chunk(k, carry):
        at = pl.ds(pl.multiple_of(k * CHUNK, CHUNK), CHUNK)
        h1[:, at] = onehot(iota((ROWS, CHUNK), 0) == ids[0:1, at])
        r1[:, at] = onehot(iota((2048, CHUNK), 0) == ids[1:2, at])
        tail_hit = iota((ROWS, CHUNK), 0) == ids[2:3, at]
        h = nn(hb[...], h1[:, at])
        r = nn(rel[...], r1[0:RELS, at])
        t = nn(tb[...], onehot(tail_hit))
        h_re, h_im = h[0:HALF], h[HALF:D]
        r_re, r_im = r[0:HALF], r[HALF:D]
        q_re = h_re * r_re - h_im * r_im
        q_im = h_re * r_im + h_im * r_re
        s0 = jnp.sum(q_re * t[0:HALF] + q_im * t[HALF:D], axis=0, keepdims=True)
        q_low = jnp.concatenate([q_re, q_im], axis=0).astype(BF16)
        ql[:, at] = q_low
        s = nn(tr[...], q_low) + logc[...]
        m = jnp.maximum(s0, jnp.max(s, axis=0, keepdims=True))
        e0 = jnp.exp(s0 - m)
        e = jnp.exp(s - m)
        z = e0 + jnp.sum(e, axis=0, keepdims=True)
        slot = iota((1, CHUNK), 1) + k * CHUNK
        valid = jnp.where(slot < count[0], 1.0, 0.0)
        g0 = valid * (e0 / z - 1.0)
        a = (e * (valid / z) + jnp.where(tail_hit, g0, 0.0)).astype(BF16)
        av[:, at] = a
        dq = nn(tb[...], a)
        d_re, d_im = dq[0:HALF], dq[HALF:D]
        dh[:, at] = jnp.concatenate(
            [d_re * r_re + d_im * r_im, d_im * r_re - d_re * r_im], axis=0
        ).astype(BF16)
        dr[:, at] = jnp.concatenate(
            [d_re * h_re + d_im * h_im, d_im * h_re - d_re * h_im], axis=0
        ).astype(BF16)
        return carry

    lax.fori_loop(0, SLOTS // CHUNK, chunk, 0)

    def relation_block(k, carry):
        rows = pl.ds(pl.multiple_of(k * QUART, QUART), QUART)
        rel_sum[k] = nt(dr[...], r1[rows, :]).astype(BF16)
        return carry

    lax.fori_loop(0, NC * NX, relation_block, 0)

    def entity_block(x, carry):
        rows = pl.ds(pl.multiple_of(x * NDOM, NDOM), NDOM)
        ent_sum[x, :, 0:NDOM] = nt(dh[...], h1[rows, :]).astype(BF16)
        ent_sum[x, :, NDOM : 2 * NDOM] = nt(ql[...], av[rows, :]).astype(BF16)
        return carry

    lax.fori_loop(0, NX, entity_block, 0)


def span(got, rel, head, relid, tail, neg, count):
    return pl.pallas_call(
        span_kernel,
        out_shape=(
            jax.ShapeDtypeStruct((NC * NX, D, QUART), BF16),
            jax.ShapeDtypeStruct((NX, D, 2 * NDOM), BF16),
        ),
        in_specs=[VMEM] * 6 + [SMEM],
        out_specs=(VMEM, VMEM),
        scratch_shapes=[
            pltpu.VMEM((8, SLOTS), I32),
            pltpu.VMEM((D, ROWS), BF16),
            pltpu.VMEM((D, ROWS), BF16),
            pltpu.VMEM((ROWS, D), BF16),
            pltpu.VMEM((ROWS, 1), F32),
            pltpu.VMEM((ROWS, SLOTS), BF16),
            pltpu.VMEM((2048, SLOTS), BF16),
            pltpu.VMEM((D, SLOTS), BF16),
            pltpu.VMEM((D, SLOTS), BF16),
            pltpu.VMEM((ROWS, SLOTS), BF16),
            pltpu.VMEM((D, SLOTS), BF16),
        ],
        compiler_params=pltpu.CompilerParams(vmem_limit_bytes=50 << 20),
        name="span_gradients",
    )(got, rel, head, relid, tail, neg, count)


def reduce_kernel(
    rel_sum, ent_sum, plan, ent_out, rel_out,
    rc, xs, rx, ys, ry, zs, rz, agz, agy, agx, agc, rex, sb1, rb1, sb2, rb2,
    s_c, r_c, s_x, r_x, s_y, r_y, s_z, r_z, s_az, r_az, s_ay, r_ay, s_ax, r_ax, s_ac, r_ac,
    s_ex, r_ex, s_b1, r_b1, s_b2, r_b2,
):
    me = Place()
    me.barrier()
    other_core = me.at(yc=me.y * NC + (1 - me.c))

    def core_copy(j):
        return remote(rel_sum.at[(1 - me.c) * NX + j], rc.at[j], s_c.at[j], r_c.at[j], other_core)

    def x_copy(dst, src):
        return remote(xs.at[dst], rx.at[src], s_x.at[dst], r_x.at[src], me.at(x=dst))

    def ent_copy(dst, src):
        return remote(ent_sum.at[dst], rex.at[src], s_ex.at[dst], r_ex.at[src], me.at(x=dst))

    def add_core(j):
        core_copy(j).wait_recv()
        xs[j] = (rel_sum[me.c * NX + j].astype(F32) + rc[j].astype(F32)).astype(BF16)

    me.others("x", lambda p: core_copy(p).start())
    core_copy(me.x).start()

    def add_and_send(p):
        add_core(p)
        x_copy(p, me.x).start()

    me.others("x", add_and_send)
    add_core(me.x)
    me.others("x", lambda p: ent_copy(p, me.x).start())
    rx[me.x] = xs[me.x]
    me.others("x", lambda p: x_copy(p, p).wait_recv())
    total = rx[0].astype(F32) + rx[1].astype(F32) + rx[2].astype(F32) + rx[3].astype(F32)
    total = total.astype(BF16)
    for y in range(NY):
        rows = min(YROWS, D - y * YROWS)
        ys[y, 0:rows] = total[y * YROWS : y * YROWS + rows]
        if rows < YPAD:
            ys[y, rows:YPAD] = jnp.zeros((YPAD - rows, QUART), BF16)

    def y_copy(dst, src):
        return remote(ys.at[dst], ry.at[src], s_y.at[dst], r_y.at[src], me.at(yc=dst * NC + me.c))

    me.others("y", lambda p: y_copy(p, me.y).start())
    ry[me.y] = ys[me.y]
    me.others("y", lambda p: y_copy(p, p).wait_recv())
    total = ry[0].astype(F32) + ry[1].astype(F32) + ry[2].astype(F32) + ry[3].astype(F32)
    total = total.astype(BF16)
    for z in range(NZ):
        i, j = z // 2, z % 2
        zs[z] = total[i * 16 : (i + 1) * 16, j * 128 : (j + 1) * 128]

    def z_copy(dst, src):
        return remote(zs.at[dst], rz.at[src], s_z.at[dst], r_z.at[src], me.at(z=dst))

    me.others("z", lambda p: z_copy(p, me.z).start())
    rz[me.z] = zs[me.z]

    mat = (2 * NDOM, 2 * NDOM)
    rex[me.x] = ent_sum[me.x]
    me.others("x", lambda p: ent_copy(p, p).wait_recv())
    mine = rex[0].astype(F32) + rex[1].astype(F32) + rex[2].astype(F32) + rex[3].astype(F32)
    row, col = iota(mat, 0), iota(mat, 1)
    half = lax.bitwise_and(row, 1)
    z_of = lax.bitwise_and(lax.shift_right_logical(row, 1), 15)
    yc_of = lax.shift_right_logical(row, 5)
    owner = (lax.shift_right_logical(yc_of, 1) * NZ + z_of) * NC + lax.bitwise_and(yc_of, 1)
    by_owner = onehot(col == half * NDOM + owner)
    sb1[...] = nt(by_owner, mine.astype(BF16)).astype(BF16).reshape(sb1.shape)

    def b1_copy(dst, src):
        return remote(sb1.at[dst], rb1.at[src], s_b1.at[dst], r_b1.at[src], me.at(yc=dst))

    me.others("yc", lambda p: b1_copy(p, me.yc).start())
    rb1[me.yc] = sb1[me.yc]

    me.others("z", lambda p: z_copy(p, p).wait_recv())
    total = rz[0].astype(F32)
    for z in range(1, NZ):
        total += rz[z].astype(F32)
    agz[me.z] = total.astype(BF16)

    def az_copy(dst, src):
        return remote(agz.at[src], agz.at[src], s_az.at[dst], r_az.at[src], me.at(z=dst))

    me.others("z", lambda p: az_copy(p, me.z).start())

    me.others("yc", lambda p: b1_copy(p, p).wait_recv())
    sb2[...] = tn(swap_zy(mat, 0), rb1[...].reshape(2 * NDOM, D)).astype(BF16).reshape(sb2.shape)

    def b2_copy(dst, src):
        return remote(sb2.at[dst], rb2.at[src], s_b2.at[dst], r_b2.at[src], me.at(z=dst))

    me.others("z", lambda p: b2_copy(p, me.z).start())
    rb2[me.z] = sb2[me.z]

    me.others("z", lambda p: az_copy(p, p).wait_recv())
    for z in range(NZ):
        i, j = z // 2, z % 2
        agy[me.y, i * 16 : (i + 1) * 16, j * 128 : (j + 1) * 128] = agz[z]

    def ay_copy(dst, src):
        return remote(agy.at[src], agy.at[src], s_ay.at[dst], r_ay.at[src], me.at(yc=dst * NC + me.c))

    me.others("y", lambda p: ay_copy(p, me.y).start())
    me.others("y", lambda p: ay_copy(p, p).wait_recv())
    for y in range(NY):
        rows = min(YROWS, D - y * YROWS)
        agx[me.x, y * YROWS : y * YROWS + rows] = agy[y, 0:rows]

    def ax_copy(dst, src):
        return remote(agx.at[src], agx.at[src], s_ax.at[dst], r_ax.at[src], me.at(x=dst))

    def ac_copy(j):
        return remote(agx.at[j], agc.at[j], s_ac.at[j], r_ac.at[j], other_core)

    me.others("x", lambda p: ax_copy(p, me.x).start())
    ac_copy(me.x).start()

    def pass_on(p):
        ax_copy(p, p).wait_recv()
        ac_copy(p).start()

    me.others("x", pass_on)

    plan_hit = jnp.concatenate(
        [onehot(iota((NDOM, NDOM), 0) == plan[h : h + 1, :]) for h in range(2)], axis=1
    )
    pick = nt(worker_major(mat, 0), plan_hit).astype(BF16)
    me.others("z", lambda p: b2_copy(p, p).wait_recv())
    ent_out[...] = tn(rb2[...].reshape(2 * NDOM, D), pick).astype(BF16)

    me.others("x", lambda p: ac_copy(p).wait_recv())
    ac_copy(me.x).wait_recv()
    first = me.c == 0
    for j in range(NX):
        low = jnp.where(first, agx[j].astype(F32), agc[j].astype(F32)).astype(BF16)
        high = jnp.where(first, agc[j].astype(F32), agx[j].astype(F32)).astype(BF16)
        rel_out[:, j * QUART : (j + 1) * QUART] = low
        start = (NX + j) * QUART
        width = min(QUART, RELS - start)
        rel_out[:, start : start + width] = high[:, 0:width]

    core_copy(me.x).wait_send()
    ac_copy(me.x).wait_send()
    for act in (
        lambda p: core_copy(p).wait_send(),
        lambda p: x_copy(p, me.x).wait_send(),
        lambda p: ent_copy(p, me.x).wait_send(),
        lambda p: ax_copy(p, me.x).wait_send(),
        lambda p: ac_copy(p).wait_send(),
    ):
        me.others("x", act)
    me.others("y", lambda p: y_copy(p, me.y).wait_send())
    me.others("y", lambda p: ay_copy(p, me.y).wait_send())
    me.others("yc", lambda p: b1_copy(p, me.yc).wait_send())
    me.others("z", lambda p: z_copy(p, me.z).wait_send())
    me.others("z", lambda p: az_copy(p, me.z).wait_send())
    me.others("z", lambda p: b2_copy(p, me.z).wait_send())


def reduce(rel_sum, ent_sum, plan):
    dma = pltpu.SemaphoreType.DMA
    block = pltpu.VMEM((NX, D, QUART), BF16)
    yblock = pltpu.VMEM((NY, YPAD, QUART), BF16)
    tile = pltpu.VMEM((NZ, 16, 128), BF16)
    b1 = pltpu.VMEM((NYC, 2 * NZ, D), BF16)
    b2 = pltpu.VMEM((NZ, 2 * NYC, D), BF16)
    sems = []
    for size in (NX, NX, NY, NZ, NZ, NY, NX, NX, NX, NYC, NZ):
        sems += [dma((size,)), dma((size,))]
    return pl.pallas_call(
        reduce_kernel,
        out_shape=(
            jax.ShapeDtypeStruct((D, NDOM), BF16),
            jax.ShapeDtypeStruct((D, RELS), BF16),
        ),
        in_specs=[VMEM] * 3,
        out_specs=(VMEM, VMEM),
        scratch_shapes=[block, block, block, yblock, yblock, tile, tile, tile, yblock, block, block, block]
        + [b1, b1, b2, b2]
        + sems,
        compiler_params=pltpu.CompilerParams(
            collective_id=1, has_side_effects=True, vmem_limit_bytes=40 << 20
        ),
        name="reduce_rows",
    )(rel_sum, ent_sum, plan)


def per_device(entity, relation, head_ids, relation_ids, tail_ids, negative_ids, span_counts, plan):
    plan_t = plan.T
    got = gather(jnp.transpose(entity, (1, 2, 0)), plan_t)
    rel_sum, ent_sum = span(
        got,
        relation.T,
        head_ids.reshape(1, SPAN),
        relation_ids.reshape(1, SPAN),
        tail_ids.reshape(1, SPAN),
        negative_ids,
        span_counts,
    )
    ent_out, rel_out = reduce(rel_sum, ent_sum, plan_t)
    return jnp.transpose(ent_out.reshape(1, D, NDOM), (2, 0, 1)), rel_out.T


def solution(mesh):
    placed = (
        P(None, "dom", None),
        P(),
        P(("dom", "rep")),
        P(("dom", "rep")),
        P(("dom", "rep")),
        P(("dom", "rep"), None),
        P(("dom", "rep")),
        P(),
    )
    return jax.shard_map(
        per_device,
        mesh=mesh,
        in_specs=placed,
        out_specs=(P(None, ("dom", "rep"), None), P()),
        check_vma=False,
    )
```

```python
import jax
import jax.numpy as jnp
from jax import lax
from jax.experimental import pallas as pl
from jax.experimental.pallas import tpu as pltpu
from jax.sharding import PartitionSpec as P

MESH = pl.DeviceIdType.MESH
F32, BF16, I32 = jnp.float32, jnp.bfloat16, jnp.int32
VMEM = pl.BlockSpec(memory_space=pltpu.VMEM)
HBM = pl.BlockSpec(memory_space=pltpu.HBM)

NY, NZ, NC, NX = 4, 16, 2, 4
NYC = NY * NC
NDOM = NY * NZ * NC
D = 400
HALF = D // 2
RELS = 2000
RELPAD = 2048
SPAN = 1000
SLOTS = 1024
CHUNK = 256
ROWS = 512
WIDE = 256
PIECES = ((0, 128), (128, 128), (256, 128), (384, 16))
NP = len(PIECES)
NH = 2
LANES = 128
XROWS = 112
XTILES = XROWS // 16
NEVER = -1e30


def nn(a, b):
    return lax.dot_general(a, b, (((1,), (0,)), ((), ())), preferred_element_type=F32)


def nt(a, b):
    return lax.dot_general(a, b, (((1,), (1,)), ((), ())), preferred_element_type=F32)


def tn(a, b):
    return lax.dot_general(a, b, (((0,), (0,)), ((), ())), preferred_element_type=F32)


def iota(shape, axis):
    return lax.broadcasted_iota(I32, shape, axis)


def onehot(hit):
    return jnp.where(hit, 1.0, 0.0).astype(BF16)


class Place:
    def __init__(self):
        dom, self.x = lax.axis_index("dom"), lax.axis_index("rep")
        self.c = lax.rem(dom, NC)
        self.z = lax.rem(lax.div(dom, NC), NZ)
        self.y = lax.div(dom, NC * NZ)
        self.yc = self.y * NC + self.c

    def at(self, z=None, y=None, yc=None, x=None):
        z = self.z if z is None else z
        x = self.x if x is None else x
        if y is not None:
            yc = y * NC + self.c
        yc = self.yc if yc is None else yc
        return {"dom": (lax.div(yc, NC) * NZ + z) * NC + lax.rem(yc, NC), "rep": x}

    def others(self, axis, body):
        size, me = {"z": (NZ, self.z), "yc": (NYC, self.yc), "x": (NX, self.x), "y": (NY, self.y)}[axis]

        def step(k, carry):
            body(lax.rem(me + k, size))
            return carry

        lax.fori_loop(1, size, step, 0)

    def greet(self, sem):
        def hello(**where):
            pl.semaphore_signal(sem, inc=1, device_id=self.at(**where), device_id_type=MESH)

        self.others("z", lambda p: hello(z=p))
        self.others("yc", lambda p: hello(yc=p))
        self.others("x", lambda p: hello(x=p))


def remote(src, dst, send, recv, where):
    return pltpu.make_async_remote_copy(
        src_ref=src, dst_ref=dst, send_sem=send, recv_sem=recv, device_id=where, device_id_type=MESH
    )


def arrived(group, sem):
    pltpu.make_async_copy(group, group, sem).wait()


SQUARE = (2 * NDOM, 2 * NDOM)


def bits(v, low, count):
    return lax.bitwise_and(lax.shift_right_logical(v, low), (1 << count) - 1)


def by_send_order():
    row, col = iota(SQUARE, 0), iota(SQUARE, 1)
    worker = (bits(row, 2, 2) * NZ + bits(row, 4, 4)) * NC + bits(row, 1, 1)
    return onehot(col == bits(row, 0, 1) * NDOM + worker)


def swap_zy():
    row, col = iota(SQUARE, 0), iota(SQUARE, 1)
    return onehot(col == bits(row, 1, 4) * 16 + bits(row, 5, 3) * 2 + bits(row, 0, 1))


def by_owner():
    row, col = iota(SQUARE, 0), iota(SQUARE, 1)
    owner = (bits(row, 6, 2) * NZ + bits(row, 1, 4)) * NC + bits(row, 5, 1)
    return onehot(col == bits(row, 0, 1) * NDOM + owner)


def kernel(
    count, ent_hbm, rel_hbm, head_hbm, relid_hbm, tail_hbm, neg_hbm, plan_hbm,
    ent_out, rel_out,
    stripe, rel, plan, raw, ids,
    snd1, rcv1, snd2, rcv2, gx,
    hb, tb, tr, logc, h1, t1, r1, ht, rt, tt, dr, dh, av, ql,
    es, rex, sb1, rb1, sb2, rb2,
    oc, rc, ys, ry, xs, rx, zs, rz, agz, agx, agxy, agxc, agyx, agyc,
    s_in, s_1, r_1, s_2, r_2, s_3, r_3,
    s_e, r_e, s_b1, r_b1, s_b2, r_b2,
    s_c, r_c, s_y, r_y, s_x, r_x, s_z, r_z, s_az, r_az,
    s_ax, r_ax, s_axy, r_axy, s_axc, r_axc, s_ay, r_ay, s_ayx, r_ayx, s_ayc, r_ayc,
):
    me = Place()
    loads = [
        pltpu.make_async_copy(plan_hbm, plan, s_in.at[0]),
        pltpu.make_async_copy(ent_hbm.at[me.x], stripe, s_in.at[1]),
        pltpu.make_async_copy(head_hbm, raw.at[0], s_in.at[2]),
        pltpu.make_async_copy(relid_hbm, raw.at[1], s_in.at[3]),
        pltpu.make_async_copy(tail_hbm, raw.at[2], s_in.at[4]),
        pltpu.make_async_copy(neg_hbm, raw.at[3], s_in.at[5]),
        pltpu.make_async_copy(rel_hbm, rel, s_in.at[6]),
    ]
    for load in loads:
        load.start()
    hello = pltpu.get_barrier_semaphore()
    me.greet(hello)

    loads[0].wait()
    loads[1].wait()
    sq = (NDOM, NDOM)
    plan_hit = jnp.concatenate([onehot(iota(sq, 0) == plan[h : h + 1, :]) for h in range(2)], axis=1)
    picked = nn(stripe[...], plan_hit).astype(BF16)
    rows = nt(by_send_order(), picked).astype(BF16)
    for p, (d, n) in enumerate(PIECES):
        snd1[p, :, :, 0:n] = rows[:, d : d + n].reshape(NZ, 2 * NYC, n)
        if n < LANES:
            snd1[p, :, :, n:] = jnp.zeros((NZ, 2 * NYC, LANES - n), BF16)

    def copy1(p, dst, src):
        return remote(snd1.at[p, dst], rcv1.at[p, src], s_1, r_1.at[p], me.at(z=dst))

    def copy2(p, dst, src):
        return remote(snd2.at[p, dst], rcv2.at[p, src], s_2, r_2.at[p], me.at(yc=dst))

    def copy3(p, dst, src):
        part = gx.at[src, pl.ds(*PIECES[p])]
        return remote(part, part, s_3, r_3.at[p], me.at(x=dst))
    pl.semaphore_wait(hello, NX + NYC + NZ - 3)
    for p in range(NP):
        me.others("z", lambda q, p=p: copy1(p, q, me.z).start())
        rcv1[p, me.z] = snd1[p, me.z]

    def over_yc(p):
        arrived(rcv1.at[p, pl.ds(0, NZ - 1)], r_1.at[p])
        turned = nn(swap_zy(), rcv1[p].reshape(2 * NDOM, LANES)).astype(BF16)
        snd2[p] = turned.reshape(NYC, 2 * NZ, LANES)
        me.others("yc", lambda q: copy2(p, q, me.yc).start())
        rcv2[p, me.yc] = snd2[p, me.yc]

    def over_x(p):
        d, n = PIECES[p]
        arrived(rcv2.at[p, pl.ds(0, NYC - 1)], r_2.at[p])
        turned = tn(rcv2[p].reshape(2 * NDOM, LANES), by_owner()).astype(BF16)
        gx[me.x, d : d + n] = turned[0:n]
        me.others("x", lambda q: copy3(p, q, me.x).start())

    def relation_rows(k):
        at = slice(k * CHUNK, (k + 1) * CHUNK)
        r1[:, at] = onehot(iota((RELPAD, CHUNK), 0) == ids[1:2, at])
        rt[:, at] = nn(rel[...], r1[0:RELS, at]).astype(BF16)
    for load in loads[2:6]:
        load.wait()
    ids[...] = jnp.full(ids.shape, -4, I32)
    for k in range(4):
        ids[k : k + 1, 0:SPAN] = raw[k]
    given = ids[...]
    place = lax.bitwise_and(given, 3) * NDOM + lax.shift_right_arithmetic(given, 2)
    ids[...] = jnp.where(iota(ids.shape, 0) == 1, given, place)
    loads[6].wait()
    relation_rows(0)
    relation_rows(1)
    over_yc(0)
    relation_rows(2)
    over_yc(1)
    over_x(0)
    relation_rows(3)
    over_yc(2)
    over_x(1)
    times = jnp.zeros((ROWS, 1), F32)
    for k in range(SLOTS // CHUNK):
        at = slice(k * CHUNK, (k + 1) * CHUNK)
        hit = iota((ROWS, CHUNK), 0) == ids[3:4, at]
        times += jnp.sum(jnp.where(hit, 1.0, 0.0), axis=1, keepdims=True)
        h1[:, at] = onehot(iota((ROWS, CHUNK), 0) == ids[0:1, at])
        t1[:, at] = onehot(iota((ROWS, CHUNK), 0) == ids[2:3, at])
    logc[...] = jnp.where(times > 0.0, jnp.log(jnp.maximum(times, 1.0)), NEVER)
    over_yc(3)
    over_x(2)
    over_x(3)
    for p, (d, n) in enumerate(PIECES):
        arrived(gx.at[pl.ds(0, NX - 1), pl.ds(d, n)], r_3.at[p])
        for x in range(NX):
            lanes = slice(x * NDOM, (x + 1) * NDOM)
            hb[d : d + n, lanes] = gx[x, d : d + n, 0:NDOM]
            tb[d : d + n, lanes] = gx[x, d : d + n, NDOM:]
        tr[:, d : d + n] = tb[d : d + n, :].T
        ht[d : d + n, :] = nn(hb[d : d + n, :], h1[...]).astype(BF16)
        tt[d : d + n, :] = nn(tb[d : d + n, :], t1[...]).astype(BF16)

    def chunk(k, carry):
        at = pl.ds(pl.multiple_of(k * CHUNK, CHUNK), CHUNK)
        h, r, t = ht[:, at].astype(F32), rt[:, at].astype(F32), tt[:, at].astype(F32)
        h_re, h_im = h[0:HALF], h[HALF:D]
        r_re, r_im = r[0:HALF], r[HALF:D]
        q_re = h_re * r_re - h_im * r_im
        q_im = h_re * r_im + h_im * r_re
        s0 = jnp.sum(q_re * t[0:HALF] + q_im * t[HALF:D], axis=0, keepdims=True)
        q_low = jnp.concatenate([q_re, q_im], axis=0).astype(BF16)
        ql[:, at] = q_low
        s = nn(tr[...], q_low) + logc[...]
        m = jnp.maximum(s0, jnp.max(s, axis=0, keepdims=True))
        e0 = jnp.exp(s0 - m)
        e = jnp.exp(s - m)
        z = e0 + jnp.sum(e, axis=0, keepdims=True)
        slot = iota((1, CHUNK), 1) + k * CHUNK
        valid = jnp.where(slot < count[0], 1.0, 0.0)
        g0 = valid * (e0 / z - 1.0)
        tail_hit = iota((ROWS, CHUNK), 0) == ids[2:3, at]
        a = (e * (valid / z) + jnp.where(tail_hit, g0, 0.0)).astype(BF16)
        av[:, at] = a
        dq = nn(tb[...], a)
        d_re, d_im = dq[0:HALF], dq[HALF:D]
        dh[:, at] = jnp.concatenate(
            [d_re * r_re + d_im * r_im, d_im * r_re - d_re * r_im], axis=0
        ).astype(BF16)
        dr[:, at] = jnp.concatenate(
            [d_re * h_re + d_im * h_im, d_im * h_re - d_re * h_im], axis=0
        ).astype(BF16)
        return carry
    lax.fori_loop(0, SLOTS // CHUNK, chunk, 0)

    def ent_copy(p, dst, src):
        part = pl.ds(*PIECES[p])
        return remote(es.at[dst, part], rex.at[src, part], s_e, r_e.at[p], me.at(x=dst))

    def b1_copy(p, dst, src):
        return remote(sb1.at[p, dst], rb1.at[p, src], s_b1, r_b1.at[p], me.at(yc=dst))

    def b2_copy(p, dst, src):
        return remote(sb2.at[p, dst], rb2.at[p, src], s_b2, r_b2.at[p], me.at(z=dst))

    other_core = me.at(yc=me.y * NC + (1 - me.c))

    def core_copy(y):
        return remote(oc.at[y], rc.at[y], s_c, r_c.at[y], other_core)

    def y_copy(dst, src):
        return remote(ys.at[dst], ry.at[src], s_y, r_y, me.at(y=dst))

    def x_copy(dst, src):
        return remote(xs.at[dst], rx.at[src], s_x, r_x, me.at(x=dst))

    def z_copy(dst, src):
        return remote(zs.at[dst], rz.at[src], s_z.at[dst], r_z, me.at(z=dst))

    def az_copy(dst, src):
        return remote(agz.at[src], agz.at[src], s_az, r_az.at[src], me.at(z=dst))

    def ax_copy(dst, src):
        return remote(agx.at[src], agx.at[src], s_ax, r_ax, me.at(x=dst))

    def axy_copy(dst, src):
        return remote(agxy.at[src], agxy.at[src], s_axy, r_axy.at[src], me.at(y=dst))

    def axc_copy(y):
        return remote(agxy.at[y], agxc.at[y], s_axc, r_axc, other_core)

    def ay_copy(dst, src):
        part = agyx.at[me.x, src]
        return remote(part, part, s_ay, r_ay, me.at(y=dst))

    def ayx_copy(dst, src):
        return remote(agyx.at[src], agyx.at[src], s_ayx, r_ayx.at[src], me.at(x=dst))

    def ayc_copy(x):
        return remote(agyx.at[x], agyc.at[x], s_ayc, r_ayc, other_core)

    def entity_block(x):
        lanes = pl.ds(pl.multiple_of(x * NDOM, NDOM), NDOM)
        es[x, :, 0:NDOM] = nt(dh[...], h1[lanes, :]).astype(BF16)
        es[x, :, NDOM : 2 * NDOM] = nt(ql[...], av[lanes, :]).astype(BF16)

    def entity_block_out(x):
        entity_block(x)
        for p in range(NP):
            ent_copy(p, x, me.x).start()

    def relation_block(c, y):
        lanes = pl.ds(pl.multiple_of((c * NY + y) * WIDE, WIDE), WIDE)
        return nt(dr[...], r1[lanes, :])

    def to_core(y):
        oc[y] = relation_block(1 - me.c, y).astype(BF16)
        core_copy(y).start()

    def with_core(y):
        block = relation_block(me.c, y)
        core_copy(y).wait_recv()
        ys[y] = (block + rc[y].astype(F32)).astype(BF16)

    def with_core_out(y):
        with_core(y)
        y_copy(y, me.y).start()

    def four(ref):
        return ref[0].astype(F32) + ref[1].astype(F32) + ref[2].astype(F32) + ref[3].astype(F32)

    def rel_x():
        ry[me.y] = ys[me.y]
        arrived(ry.at[pl.ds(0, NY - 1)], r_y)
        total = four(ry).astype(BF16)
        for x in range(NX):
            n = min(XROWS, D - x * XROWS)
            xs[x, 0:n] = total[x * XROWS : x * XROWS + n]
            if n < XROWS:
                xs[x, n:] = jnp.zeros((XROWS - n, WIDE), BF16)
        me.others("x", lambda q: x_copy(q, me.x).start())

    def tiles(body):
        def step(i, carry):
            z = lax.div(i, XTILES) * 8 + lax.rem(i, XTILES)

            @pl.when(z != me.z)
            def _():
                body(z)

            return carry

        lax.fori_loop(0, NH * XTILES, step, 0)

    def rel_z():
        rx[me.x] = xs[me.x]
        arrived(rx.at[pl.ds(0, NX - 1)], r_x)
        total = four(rx).astype(BF16)
        for h in range(NH):
            half = total[:, h * LANES : (h + 1) * LANES]
            zs[h * 8 : h * 8 + XTILES] = half.reshape(XTILES, 16, LANES)
        tiles(lambda q: z_copy(q, me.z).start())

    owns = lax.rem(me.z, 8) < XTILES

    def rel_az():
        @pl.when(owns)
        def _():
            rz[me.z] = zs[me.z]
            arrived(rz.at[pl.ds(0, NZ - 1)], r_z)
            total = rz[0].astype(F32)
            for z in range(1, NZ):
                total += rz[z].astype(F32)
            agz[me.z] = total.astype(BF16)
            me.others("z", lambda q: az_copy(q, me.z).start())

    def rel_back1():
        tiles(lambda q: az_copy(q, q).wait_recv())
        agx[me.x] = agz[0:XTILES].reshape(XROWS, LANES)
        me.others("x", lambda q: ax_copy(q, me.x).start())
        agyx[me.x, me.y] = agz[8 : 8 + XTILES].reshape(XROWS, LANES)
        me.others("y", lambda q: ay_copy(q, me.y).start())

    def rel_back2():
        arrived(agx.at[pl.ds(0, NX - 1)], r_ax)
        for x in range(NX):
            n = min(XROWS, D - x * XROWS)
            agxy[me.y, x * XROWS : x * XROWS + n] = agx[x, 0:n]
        me.others("y", lambda q: axy_copy(q, me.y).start())
        arrived(agyx.at[0, pl.ds(0, NY - 1)], r_ay)
        me.others("x", lambda q: ayx_copy(q, me.x).start())
        axc_copy(me.y).start()
        ayc_copy(me.x).start()

    def rel_core():
        def step(k, carry):
            y = lax.rem(me.y + k, NY)
            axy_copy(y, y).wait_recv()
            axc_copy(y).start()
            x = lax.rem(me.x + k, NX)
            ayx_copy(x, x).wait_recv()
            ayc_copy(x).start()
            return carry

        lax.fori_loop(1, NX, step, 0)

    def rel_place(c, sub, block, rows):
        start = (c * NY * NH + sub) * LANES
        n = min(LANES, RELS - start)
        rel_out[rows[0] : rows[1], start : start + n] = block.astype(BF16)[:, 0:n]

    def rel_done():
        arrived(agxc, r_axc)
        arrived(agyc, r_ayc)
        first = me.c == 0

        def both(here, there, sub, rows):
            here, there = here.astype(F32), there.astype(F32)
            rel_place(0, sub, jnp.where(first, here, there), rows)
            rel_place(1, sub, jnp.where(first, there, here), rows)

        for y in range(NY):
            both(agxy[y], agxc[y], y * NH, (0, D))
            for x in range(NX):
                n = min(XROWS, D - x * XROWS)
                both(agyx[x, y, 0:n], agyc[x, y, 0:n], y * NH + 1, (x * XROWS, x * XROWS + n))

    def ent_yc(p):
        d, n = PIECES[p]
        rex[me.x, d : d + n] = es[me.x, d : d + n]
        arrived(rex.at[pl.ds(0, NX - 1), pl.ds(d, n)], r_e.at[p])
        total = sum(rex[x, d : d + n].astype(F32) for x in range(NX)).astype(BF16)
        turned = nt(by_owner(), total).astype(BF16).reshape(NYC, 2 * NZ, n)
        sb1[p, :, :, 0:n] = turned
        if n < LANES:
            sb1[p, :, :, n:] = jnp.zeros((NYC, 2 * NZ, LANES - n), BF16)
        me.others("yc", lambda q: b1_copy(p, q, me.yc).start())
        rb1[p, me.yc] = sb1[p, me.yc]

    def ent_rows(p):
        arrived(rb1.at[p, pl.ds(0, NYC - 1)], r_b1.at[p])
        turned = tn(swap_zy(), rb1[p].reshape(2 * NDOM, LANES)).astype(BF16)
        sb2[p] = turned.reshape(NZ, 2 * NYC, LANES)
        rb2[p, me.z] = sb2[p, me.z]

    def ent_z(p):
        me.others("z", lambda q: b2_copy(p, q, me.z).start())

    def ent_done(p, pick):
        d, n = PIECES[p]
        arrived(rb2.at[p, pl.ds(0, NZ - 1)], r_b2.at[p])
        ent_out[d : d + n, :] = tn(rb2[p].reshape(2 * NDOM, LANES), pick)[0:n].astype(BF16)
    me.others("x", entity_block_out)
    entity_block(me.x)
    me.others("y", to_core)
    to_core(me.y)
    me.others("y", with_core_out)
    with_core(me.y)
    for p in range(NP):
        ent_yc(p)
    for p in range(NP):
        ent_rows(p)
    ent_z(0)
    rel_x()
    rel_z()
    parts = jnp.concatenate([onehot(iota(sq, 0) == plan[h : h + 1, :]) for h in range(2)], axis=1)
    pick = nt(by_send_order(), parts).astype(BF16)
    rel_az()
    rel_back1()
    for p in range(1, NP):
        ent_z(p)
    rel_back2()
    rel_core()
    for p in range(NP):
        ent_done(p, pick)
    rel_done()
    arrived(snd1.at[:, pl.ds(0, NZ - 1)], s_1)
    arrived(snd2.at[:, pl.ds(0, NYC - 1)], s_2)
    arrived(gx.at[pl.ds(0, NX - 1)], s_3)
    arrived(es.at[pl.ds(0, NX - 1)], s_e)
    arrived(sb1.at[:, pl.ds(0, NYC - 1)], s_b1)
    arrived(sb2.at[:, pl.ds(0, NZ - 1)], s_b2)
    arrived(oc, s_c)
    arrived(ys.at[pl.ds(0, NY - 1)], s_y)
    arrived(xs.at[pl.ds(0, NX - 1)], s_x)
    arrived(agx.at[pl.ds(0, NX - 1)], s_ax)
    arrived(agyx.at[0, pl.ds(0, NY - 1)], s_ay)
    arrived(agxy.at[pl.ds(0, NY - 1)], s_axy)
    arrived(agyx.at[pl.ds(0, NX - 1)], s_ayx)
    arrived(agxc, s_axc)
    arrived(agyc, s_ayc)
    tiles(lambda q: z_copy(q, me.z).wait_send())

    @pl.when(owns)
    def _():
        arrived(agz.at[pl.ds(0, NZ - 1)], s_az)


def scratch():
    def bf16(*shape):
        return pltpu.VMEM(shape, BF16)

    dma = pltpu.SemaphoreType.DMA

    by_z, by_yc = bf16(NP, NZ, 2 * NYC, LANES), bf16(NP, NYC, 2 * NZ, LANES)
    block, slots, half = bf16(NX, D, WIDE), bf16(D, SLOTS), bf16(NY, D, LANES)
    small, tile = bf16(NX, XROWS, WIDE), bf16(NZ, 16, LANES)
    thin, quads = bf16(NX, XROWS, LANES), bf16(NX, NY, XROWS, LANES)
    return (
        [bf16(D, NDOM), bf16(D, RELS), pltpu.VMEM((2, NDOM), I32)]
        + [pltpu.VMEM((4, 1, SPAN), I32), pltpu.VMEM((8, SLOTS), I32)]
        + [by_z, by_z, by_yc, by_yc, block]
        + [bf16(D, ROWS), bf16(D, ROWS), bf16(ROWS, D), pltpu.VMEM((ROWS, 1), F32)]
        + [bf16(ROWS, SLOTS), bf16(ROWS, SLOTS), bf16(RELPAD, SLOTS)]
        + [slots, slots, slots, slots, slots, bf16(ROWS, SLOTS), slots]
        + [block, block, by_yc, by_yc, by_z, by_z]
        + [block, block, block, block, small, small, tile, tile, tile]
        + [thin, half, half, quads, quads]
        + [dma((7,))]
        + [dma, dma((NP,))] * 6
        + [dma, dma((NY,)), dma, dma, dma, dma, dma((NZ,)), dma, dma, dma((NZ,))]
        + [dma, dma, dma, dma((NY,)), dma, dma]
        + [dma, dma, dma, dma((NX,)), dma, dma]
    )


def per_device(entity, relation, head_ids, relation_ids, tail_ids, negative_ids, span_counts, plan):
    ent_out, rel_out = pl.pallas_call(
        kernel,
        out_shape=(
            jax.ShapeDtypeStruct((D, NDOM), BF16),
            jax.ShapeDtypeStruct((D, RELS), BF16),
        ),
        in_specs=[pl.BlockSpec(memory_space=pltpu.SMEM)] + [HBM] * 7,
        out_specs=(VMEM, VMEM),
        scratch_shapes=scratch(),
        compiler_params=pltpu.CompilerParams(
            collective_id=0, has_side_effects=True, vmem_limit_bytes=40 << 20
        ),
        name="bucket_round",
    )(
        span_counts,
        *(
            pltpu.with_memory_space_constraint(v, pltpu.HBM)
            for v in (
                jnp.transpose(entity, (1, 2, 0)),
                relation.T,
                head_ids.reshape(1, SPAN),
                relation_ids.reshape(1, SPAN),
                tail_ids.reshape(1, SPAN),
                negative_ids,
                plan.T,
            )
        ),
    )
    return jnp.transpose(ent_out.reshape(1, D, NDOM), (2, 0, 1)), rel_out.T


def solution(mesh):
    placed = (
        P(None, "dom", None),
        P(),
        P(("dom", "rep")),
        P(("dom", "rep")),
        P(("dom", "rep")),
        P(("dom", "rep"), None),
        P(("dom", "rep")),
        P(),
    )
    return jax.shard_map(
        per_device,
        mesh=mesh,
        in_specs=placed,
        out_specs=(P(None, ("dom", "rep"), None), P()),
        check_vma=False,
    )
```

```python
import jax
import jax.numpy as jnp
from jax import lax
from jax.experimental import pallas as pl
from jax.experimental.pallas import tpu as pltpu
from jax.sharding import PartitionSpec as P

MESH = pl.DeviceIdType.MESH
F32, BF16, I32 = jnp.float32, jnp.bfloat16, jnp.int32
VMEM = pl.BlockSpec(memory_space=pltpu.VMEM)
HBM = pl.BlockSpec(memory_space=pltpu.HBM)

NY, NZ, NC, NX = 4, 16, 2, 4
NYC = NY * NC
NDOM = NY * NZ * NC
D = 400
HALF = D // 2
RELS = 2000
RELPAD = 2048
SPAN = 1000
SLOTS = 1024
CHUNK = 256
ROWS = 512
WIDE = 256
PIECES = ((0, 256), (256, 128), (384, 16))
NP = len(PIECES)
BACK = ((0, 256), (256, 144))
NB = len(BACK)
NH = 2
LANES = 128
XROWS = 112
XTILES = XROWS // 16
NEVER = -1e30


def nn(a, b):
    return lax.dot_general(a, b, (((1,), (0,)), ((), ())), preferred_element_type=F32)


def nt(a, b):
    return lax.dot_general(a, b, (((1,), (1,)), ((), ())), preferred_element_type=F32)


def tn(a, b):
    return lax.dot_general(a, b, (((0,), (0,)), ((), ())), preferred_element_type=F32)


def iota(shape, axis):
    return lax.broadcasted_iota(I32, shape, axis)


def onehot(hit):
    return jnp.where(hit, 1.0, 0.0).astype(BF16)


class Place:
    def __init__(self):
        dom, self.x = lax.axis_index("dom"), lax.axis_index("rep")
        self.c = lax.rem(dom, NC)
        self.z = lax.rem(lax.div(dom, NC), NZ)
        self.y = lax.div(dom, NC * NZ)
        self.yc = self.y * NC + self.c

    def at(self, z=None, y=None, yc=None, x=None):
        z = self.z if z is None else z
        x = self.x if x is None else x
        if y is not None:
            yc = y * NC + self.c
        yc = self.yc if yc is None else yc
        return {"dom": (lax.div(yc, NC) * NZ + z) * NC + lax.rem(yc, NC), "rep": x}

    def others(self, axis, body):
        size, me = {"z": (NZ, self.z), "yc": (NYC, self.yc), "x": (NX, self.x), "y": (NY, self.y)}[axis]

        def step(k, carry):
            away = size // 2 + lax.div(k, 2) * (1 - 2 * lax.rem(k, 2))
            body(lax.rem(me + away, size))
            return carry

        lax.fori_loop(1, size, step, 0)

    def greet(self, sem):
        def hello(**where):
            pl.semaphore_signal(sem, inc=1, device_id=self.at(**where), device_id_type=MESH)

        self.others("z", lambda p: hello(z=p))
        self.others("yc", lambda p: hello(yc=p))
        self.others("x", lambda p: hello(x=p))


def remote(src, dst, send, recv, where):
    return pltpu.make_async_remote_copy(
        src_ref=src, dst_ref=dst, send_sem=send, recv_sem=recv, device_id=where, device_id_type=MESH
    )


def arrived(group, sem):
    pltpu.make_async_copy(group, group, sem).wait()


SQUARE = (2 * NDOM, 2 * NDOM)


def bits(v, low, count):
    return lax.bitwise_and(lax.shift_right_logical(v, low), (1 << count) - 1)


def by_send_order():
    row, col = iota(SQUARE, 0), iota(SQUARE, 1)
    worker = (bits(row, 2, 2) * NZ + bits(row, 4, 4)) * NC + bits(row, 1, 1)
    return onehot(col == bits(row, 0, 1) * NDOM + worker)


def swap_zy():
    row, col = iota(SQUARE, 0), iota(SQUARE, 1)
    return onehot(col == bits(row, 1, 4) * 16 + bits(row, 5, 3) * 2 + bits(row, 0, 1))


def by_owner():
    row, col = iota(SQUARE, 0), iota(SQUARE, 1)
    owner = (bits(row, 6, 2) * NZ + bits(row, 1, 4)) * NC + bits(row, 5, 1)
    return onehot(col == bits(row, 0, 1) * NDOM + owner)


def kernel(
    count, ent_hbm, rel_hbm, head_hbm, relid_hbm, tail_hbm, neg_hbm, plan_hbm,
    ent_out, rel_out,
    stripe, rel, plan, raw, ids,
    snd1, rcv1, snd2, rcv2, gx,
    hb, tb, tr, logc, h1, t1, r1, ht, rt, tt, dr, dh, av, ql,
    es, rex, sb1, rb1, sb2, rb2,
    oc, rc, asend, aland, bsend, bland, zs, rz, agz, dback, fback, gback,
    s_in, s_1, r_1, s_2, r_2, s_3, r_3,
    s_e, r_e, s_b1, r_b1, s_b2, r_b2,
    s_c, r_c, s_a, r_a, s_b, r_b, s_z, r_z, s_az, r_az, s_d, r_d, s_f, r_f, s_g, r_g,
):
    me = Place()
    loads = [
        pltpu.make_async_copy(plan_hbm, plan, s_in.at[0]),
        pltpu.make_async_copy(ent_hbm.at[me.x], stripe, s_in.at[1]),
        pltpu.make_async_copy(head_hbm, raw.at[0], s_in.at[2]),
        pltpu.make_async_copy(relid_hbm, raw.at[1], s_in.at[3]),
        pltpu.make_async_copy(tail_hbm, raw.at[2], s_in.at[4]),
        pltpu.make_async_copy(neg_hbm, raw.at[3], s_in.at[5]),
        pltpu.make_async_copy(rel_hbm, rel, s_in.at[6]),
    ]
    for load in loads:
        load.start()
    hello = pltpu.get_barrier_semaphore()
    me.greet(hello)

    loads[0].wait()
    loads[1].wait()
    sq = (NDOM, NDOM)
    plan_hit = jnp.concatenate([onehot(iota(sq, 0) == plan[h : h + 1, :]) for h in range(2)], axis=1)
    picked = nn(stripe[...], plan_hit).astype(BF16)
    rows = nt(by_send_order(), picked).astype(BF16)
    for p, (d, n) in enumerate(PIECES):
        snd1[p][...] = rows[:, d : d + n].reshape(NZ, 2 * NYC, n)

    def copy1(p, dst, src):
        return remote(snd1[p].at[dst], rcv1[p].at[src], s_1.at[p], r_1.at[p], me.at(z=dst))

    def copy2(p, dst, src):
        return remote(snd2[p].at[dst], rcv2[p].at[src], s_2.at[p], r_2.at[p], me.at(yc=dst))

    def copy3(p, dst, src):
        part = gx.at[src, pl.ds(*PIECES[p])]
        return remote(part, part, s_3, r_3.at[p], me.at(x=dst))
    pl.semaphore_wait(hello, NX + NYC + NZ - 3)
    for p in range(NP):
        me.others("z", lambda q, p=p: copy1(p, q, me.z).start())
        rcv1[p][me.z] = snd1[p][me.z]

    def over_yc(p):
        arrived(rcv1[p].at[pl.ds(0, NZ - 1)], r_1.at[p])
        turned = nn(swap_zy(), rcv1[p][...].reshape(2 * NDOM, PIECES[p][1])).astype(BF16)
        snd2[p][...] = turned.reshape(NYC, 2 * NZ, PIECES[p][1])
        me.others("yc", lambda q: copy2(p, q, me.yc).start())
        rcv2[p][me.yc] = snd2[p][me.yc]

    def over_x(p):
        d, n = PIECES[p]
        arrived(rcv2[p].at[pl.ds(0, NYC - 1)], r_2.at[p])
        turned = tn(rcv2[p][...].reshape(2 * NDOM, n), by_owner()).astype(BF16)
        gx[me.x, d : d + n] = turned
        me.others("x", lambda q: copy3(p, q, me.x).start())

    def relation_rows(k):
        at = slice(k * CHUNK, (k + 1) * CHUNK)
        r1[at, :] = onehot(iota((CHUNK, RELPAD), 1) == columns[at, 1:2])
        rt[:, at] = nt(rel[...], r1[at, 0:RELS]).astype(BF16)
    for load in loads[2:6]:
        load.wait()
    ids[...] = jnp.full(ids.shape, -4, I32)
    for k in range(4):
        ids[k : k + 1, 0:SPAN] = raw[k]
    given = ids[...]
    place = lax.bitwise_and(given, 3) * NDOM + lax.shift_right_arithmetic(given, 2)
    ids[...] = jnp.where(iota(ids.shape, 0) == 1, given, place)
    columns = ids[...].T
    loads[6].wait()
    for k in range(SLOTS // CHUNK):
        relation_rows(k)
    times = jnp.zeros((ROWS, 1), F32)
    for k in range(SLOTS // CHUNK):
        at = slice(k * CHUNK, (k + 1) * CHUNK)
        hit = iota((ROWS, CHUNK), 0) == ids[3:4, at]
        times += jnp.sum(jnp.where(hit, 1.0, 0.0), axis=1, keepdims=True)
        h1[:, at] = onehot(iota((ROWS, CHUNK), 0) == ids[0:1, at])
        t1[:, at] = onehot(iota((ROWS, CHUNK), 0) == ids[2:3, at])
    logc[...] = jnp.where(times > 0.0, jnp.log(jnp.maximum(times, 1.0)), NEVER)
    def rows_in(p):
        d, n = PIECES[p]
        arrived(gx.at[pl.ds(0, NX - 1), pl.ds(d, n)], r_3.at[p])
        for x in range(NX):
            lanes = slice(x * NDOM, (x + 1) * NDOM)
            hb[d : d + n, lanes] = gx[x, d : d + n, 0:NDOM]
            tb[d : d + n, lanes] = gx[x, d : d + n, NDOM:]
        tr[:, d : d + n] = tb[d : d + n, :].T
        ht[d : d + n, :] = nn(hb[d : d + n, :], h1[...]).astype(BF16)
        tt[d : d + n, :] = nn(tb[d : d + n, :], t1[...]).astype(BF16)
    over_yc(0)
    over_yc(1)
    over_x(0)
    over_yc(2)
    over_x(1)
    over_x(2)
    rows_in(0)
    rows_in(1)
    rows_in(2)

    def chunk(k, carry):
        at = pl.ds(pl.multiple_of(k * CHUNK, CHUNK), CHUNK)
        h, r, t = ht[:, at].astype(F32), rt[:, at].astype(F32), tt[:, at].astype(F32)
        h_re, h_im = h[0:HALF], h[HALF:D]
        r_re, r_im = r[0:HALF], r[HALF:D]
        q_re = h_re * r_re - h_im * r_im
        q_im = h_re * r_im + h_im * r_re
        s0 = jnp.sum(q_re * t[0:HALF] + q_im * t[HALF:D], axis=0, keepdims=True)
        q_low = jnp.concatenate([q_re, q_im], axis=0).astype(BF16)
        ql[:, at] = q_low
        s = nn(tr[...], q_low) + logc[...]
        m = jnp.maximum(s0, jnp.max(s, axis=0, keepdims=True))
        e0 = jnp.exp(s0 - m)
        e = jnp.exp(s - m)
        z = e0 + jnp.sum(e, axis=0, keepdims=True)
        slot = iota((1, CHUNK), 1) + k * CHUNK
        valid = jnp.where(slot < count[0], 1.0, 0.0)
        g0 = valid * (e0 / z - 1.0)
        tail_hit = iota((ROWS, CHUNK), 0) == ids[2:3, at]
        a = (e * (valid / z) + jnp.where(tail_hit, g0, 0.0)).astype(BF16)
        av[:, at] = a
        dq = nn(tb[...], a)
        d_re, d_im = dq[0:HALF], dq[HALF:D]
        dh[:, at] = jnp.concatenate(
            [d_re * r_re + d_im * r_im, d_im * r_re - d_re * r_im], axis=0
        ).astype(BF16)
        dr[:, at] = jnp.concatenate(
            [d_re * h_re + d_im * h_im, d_im * h_re - d_re * h_im], axis=0
        ).astype(BF16)
        return carry
    lax.fori_loop(0, SLOTS // CHUNK, chunk, 0, unroll=True)

    def ent_copy(p, dst, src):
        part = pl.ds(*BACK[p])
        return remote(es.at[dst, part], rex.at[src, part], s_e, r_e.at[p], me.at(x=dst))

    def b1_copy(p, dst, src):
        return remote(sb1[p].at[dst], rb1[p].at[src], s_b1.at[p], r_b1.at[p], me.at(yc=dst))

    def b2_copy(p, dst, src):
        return remote(sb2[p].at[dst], rb2[p].at[src], s_b2.at[p], r_b2.at[p], me.at(z=dst))

    other_core = me.at(yc=me.y * NC + (1 - me.c))

    def core_copy(j):
        return remote(oc.at[j], rc.at[j], s_c, r_c.at[j], other_core)

    axes = (("y", "x"), ("x", "y"))
    index = {"x": me.x, "y": me.y}

    def copy_a(h, dst, src):
        return remote(asend.at[h, dst], aland.at[h, src], s_a.at[h], r_a.at[h], me.at(**{axes[h][0]: dst}))

    def copy_b(h, dst, src):
        return remote(bsend.at[h, dst], bland.at[h, src], s_b.at[h], r_b.at[h], me.at(**{axes[h][1]: dst}))

    def z_copy(dst, src):
        return remote(zs.at[dst], rz.at[src], s_z.at[dst], r_z, me.at(z=dst))

    def az_copy(dst, src):
        return remote(agz.at[src], agz.at[src], s_az, r_az.at[src], me.at(z=dst))

    def copy_d(h, dst, src):
        part = dback.at[h, src]
        return remote(part, part, s_d.at[h], r_d.at[h], me.at(**{axes[h][1]: dst}))

    def copy_f(h, dst, src):
        part = fback.at[h, src]
        return remote(part, part, s_f.at[h], r_f.at[h, src], me.at(**{axes[h][0]: dst}))

    def copy_g(h, j):
        return remote(fback.at[h, j], gback.at[h, j], s_g.at[h], r_g.at[h], other_core)

    def entity_block(x):
        lanes = pl.ds(pl.multiple_of(x * NDOM, NDOM), NDOM)
        es[x, :, 0:NDOM] = nt(dh[...], h1[lanes, :]).astype(BF16)
        es[x, :, NDOM : 2 * NDOM] = nt(ql[...], av[lanes, :]).astype(BF16)

    def entity_out(x):
        for p in range(NB):
            ent_copy(p, x, me.x).start()

    def relation_block(c, y):
        lanes = pl.ds(pl.multiple_of((c * NY + y) * WIDE, WIDE), WIDE)
        return nn(dr[...], r1[:, lanes])

    def to_core(j):
        oc[j] = relation_block(1 - me.c, j).astype(BF16)
        core_copy(j).start()

    def with_core(j):
        block = relation_block(me.c, j)
        core_copy(j).wait_recv()
        block = (block + rc[j].astype(F32)).astype(BF16)
        for h in range(NH):
            asend[h, j] = block[:, h * LANES : (h + 1) * LANES]

            @pl.when(j != index[axes[h][0]])
            def _(h=h):
                copy_a(h, j, index[axes[h][0]]).start()

    def each(body):
        def step(k, carry):
            body(lax.rem(me.y + k, NY))
            return carry

        lax.fori_loop(1, NY + 1, step, 0)

    def four(ref, h):
        return sum(ref[h, j].astype(F32) for j in range(NY))

    def rel_second(h):
        first, second = axes[h]
        aland[h, index[first]] = asend[h, index[first]]
        arrived(aland.at[h, pl.ds(0, NY - 1)], r_a.at[h])
        total = four(aland, h).astype(BF16)
        for j in range(NX):
            n = min(XROWS, D - j * XROWS)
            bsend[h, j, 0:n] = total[j * XROWS : j * XROWS + n]
            if n < XROWS:
                bsend[h, j, n:] = jnp.zeros((XROWS - n, LANES), BF16)
        me.others(second, lambda q: copy_b(h, q, index[second]).start())

    def tiles(body, parts=range(NH)):
        def step(i, carry):
            z = lax.div(i, XTILES) * 8 + lax.rem(i, XTILES)

            @pl.when(z != me.z)
            def _():
                body(z)

            return carry

        lax.fori_loop(parts[0] * XTILES, (parts[-1] + 1) * XTILES, step, 0)

    def rel_z(h):
        second = axes[h][1]
        bland[h, index[second]] = bsend[h, index[second]]
        arrived(bland.at[h, pl.ds(0, NX - 1)], r_b.at[h])
        zs[h * 8 : h * 8 + XTILES] = four(bland, h).astype(BF16).reshape(XTILES, 16, LANES)
        tiles(lambda q: z_copy(q, me.z).start(), (h,))

    owns = lax.rem(me.z, 8) < XTILES

    def rel_az():
        @pl.when(owns)
        def _():
            rz[me.z] = zs[me.z]
            arrived(rz.at[pl.ds(0, NZ - 1)], r_z)
            total = rz[0].astype(F32)
            for z in range(1, NZ):
                total += rz[z].astype(F32)
            agz[me.z] = total.astype(BF16)
            me.others("z", lambda q: az_copy(q, me.z).start())

    def rel_back1(h):
        second = axes[h][1]
        tiles(lambda q: az_copy(q, q).wait_recv(), (h,))
        dback[h, index[second]] = agz[h * 8 : h * 8 + XTILES].reshape(XROWS, LANES)
        me.others(second, lambda q: copy_d(h, q, index[second]).start())

    def rel_back2(h):
        first = axes[h][0]
        arrived(dback.at[h, pl.ds(0, NX - 1)], r_d.at[h])
        for j in range(NX):
            n = min(XROWS, D - j * XROWS)
            fback[h, index[first], j * XROWS : j * XROWS + n] = dback[h, j, 0:n]
        me.others(first, lambda q: copy_f(h, q, index[first]).start())
        copy_g(h, index[first]).start()

    def rel_core():
        def step(k, carry):
            for h in range(NH):
                j = lax.rem(index[axes[h][0]] + k, NX)
                copy_f(h, j, j).wait_recv()
                copy_g(h, j).start()
            return carry

        lax.fori_loop(1, NX, step, 0)

    def rel_done():
        low = me.c == 0
        for h in range(NH):
            arrived(gback.at[h], r_g.at[h])
            for j in range(NY):
                here, there = fback[h, j].astype(F32), gback[h, j].astype(F32)
                for c in range(NC):
                    start = ((c * NY + j) * NH + h) * LANES
                    n = min(LANES, RELS - start)
                    block = jnp.where(low, here, there) if c == 0 else jnp.where(low, there, here)
                    rel_out[:, start : start + n] = block.astype(BF16)[:, 0:n]

    def ent_yc(p):
        d, n = BACK[p]
        rex[me.x, d : d + n] = es[me.x, d : d + n]
        arrived(rex.at[pl.ds(0, NX - 1), pl.ds(d, n)], r_e.at[p])
        total = sum(rex[x, d : d + n].astype(F32) for x in range(NX)).astype(BF16)
        turned = nt(by_owner(), total).astype(BF16).reshape(NYC, 2 * NZ, n)
        sb1[p][...] = turned
        me.others("yc", lambda q: b1_copy(p, q, me.yc).start())
        rb1[p][me.yc] = sb1[p][me.yc]

    def ent_rows(p):
        arrived(rb1[p].at[pl.ds(0, NYC - 1)], r_b1.at[p])
        turned = tn(swap_zy(), rb1[p][...].reshape(2 * NDOM, BACK[p][1])).astype(BF16)
        sb2[p][...] = turned.reshape(NZ, 2 * NYC, BACK[p][1])
        rb2[p][me.z] = sb2[p][me.z]

    def ent_z(p):
        me.others("z", lambda q: b2_copy(p, q, me.z).start())

    def ent_done(p, pick):
        d, n = BACK[p]
        arrived(rb2[p].at[pl.ds(0, NZ - 1)], r_b2.at[p])
        ent_out[d : d + n, :] = tn(rb2[p][...].reshape(2 * NDOM, n), pick).astype(BF16)
    each(to_core)
    each(with_core)
    me.others("x", entity_block)
    entity_block(me.x)
    parts = jnp.concatenate([onehot(iota(sq, 0) == plan[h : h + 1, :]) for h in range(2)], axis=1)
    pick = nt(by_send_order(), parts).astype(BF16)
    for h in range(NH):
        rel_second(h)
    me.others("x", entity_out)
    for h in range(NH):
        rel_z(h)
    for p in range(NB):
        ent_yc(p)
    rel_az()
    for p in range(NB):
        ent_rows(p)
        ent_z(p)
    for h in range(NH):
        rel_back1(h)
    for h in range(NH):
        rel_back2(h)
    rel_core()
    for p in range(NB):
        ent_done(p, pick)
    rel_done()
    arrived(gx.at[pl.ds(0, NX - 1)], s_3)
    arrived(es.at[pl.ds(0, NX - 1)], s_e)
    for p in range(NP):
        arrived(snd1[p].at[pl.ds(0, NZ - 1)], s_1.at[p])
        arrived(snd2[p].at[pl.ds(0, NYC - 1)], s_2.at[p])
    for p in range(NB):
        arrived(sb1[p].at[pl.ds(0, NYC - 1)], s_b1.at[p])
        arrived(sb2[p].at[pl.ds(0, NZ - 1)], s_b2.at[p])
    arrived(oc, s_c)
    for h in range(NH):
        arrived(asend.at[h, pl.ds(0, NY - 1)], s_a.at[h])
        arrived(bsend.at[h, pl.ds(0, NX - 1)], s_b.at[h])
        arrived(dback.at[h, pl.ds(0, NX - 1)], s_d.at[h])
        arrived(fback.at[h, pl.ds(0, NY - 1)], s_f.at[h])
        arrived(gback.at[h], s_g.at[h])
    tiles(lambda q: z_copy(q, me.z).wait_send())

    @pl.when(owns)
    def _():
        arrived(agz.at[pl.ds(0, NZ - 1)], s_az)


def scratch():
    def bf16(*shape):
        return pltpu.VMEM(shape, BF16)

    dma = pltpu.SemaphoreType.DMA

    def rows(pieces, *lead):
        return tuple(bf16(*lead, n) for _, n in pieces)

    by_z, by_yc = rows(PIECES, NZ, 2 * NYC), rows(PIECES, NYC, 2 * NZ)
    back_z, back_yc = rows(BACK, NZ, 2 * NYC), rows(BACK, NYC, 2 * NZ)
    block, slots, tile = bf16(NX, D, WIDE), bf16(D, SLOTS), bf16(NZ, 16, LANES)
    half, thin = bf16(NH, NY, D, LANES), bf16(NH, NX, XROWS, LANES)
    hops = [dma((NP,)), dma((NP,))]
    sides = [dma((NH,)), dma((NH,))]
    return (
        [bf16(D, NDOM), bf16(D, RELS), pltpu.VMEM((2, NDOM), I32)]
        + [pltpu.VMEM((4, 1, SPAN), I32), pltpu.VMEM((8, SLOTS), I32)]
        + [by_z, by_z, by_yc, by_yc, block]
        + [bf16(D, ROWS), bf16(D, ROWS), bf16(ROWS, D), pltpu.VMEM((ROWS, 1), F32)]
        + [bf16(ROWS, SLOTS), bf16(ROWS, SLOTS), bf16(SLOTS, RELPAD)]
        + [slots, slots, slots, slots, slots, bf16(ROWS, SLOTS), slots]
        + [block, block, back_yc, back_yc, back_z, back_z]
        + [block, block, half, half, thin, thin, tile, tile, tile, thin, half, half]
        + [dma((7,))]
        + hops * 2
        + [dma, dma((NP,)), dma, dma((NB,))]
        + [dma((NB,))] * 4
        + [dma, dma((NY,))]
        + sides * 2
        + [dma((NZ,)), dma, dma, dma((NZ,))]
        + sides
        + [dma((NH,)), dma((NH, NY))]
        + sides
    )


def per_device(entity, relation, head_ids, relation_ids, tail_ids, negative_ids, span_counts, plan):
    ent_out, rel_out = pl.pallas_call(
        kernel,
        out_shape=(
            jax.ShapeDtypeStruct((D, NDOM), BF16),
            jax.ShapeDtypeStruct((D, RELS), BF16),
        ),
        in_specs=[pl.BlockSpec(memory_space=pltpu.SMEM)] + [HBM] * 7,
        out_specs=(VMEM, VMEM),
        scratch_shapes=scratch(),
        compiler_params=pltpu.CompilerParams(
            collective_id=0, has_side_effects=True, vmem_limit_bytes=40 << 20
        ),
        name="bucket_round",
    )(
        span_counts,
        *(
            pltpu.with_memory_space_constraint(v, pltpu.HBM)
            for v in (
                jnp.transpose(entity, (1, 2, 0)),
                relation.T,
                head_ids.reshape(1, SPAN),
                relation_ids.reshape(1, SPAN),
                tail_ids.reshape(1, SPAN),
                negative_ids,
                plan.T,
            )
        ),
    )
    return jnp.transpose(ent_out.reshape(1, D, NDOM), (2, 0, 1)), rel_out.T


def solution(mesh):
    placed = (
        P(None, "dom", None),
        P(),
        P(("dom", "rep")),
        P(("dom", "rep")),
        P(("dom", "rep")),
        P(("dom", "rep"), None),
        P(("dom", "rep")),
        P(),
    )
    return jax.shard_map(
        per_device,
        mesh=mesh,
        in_specs=placed,
        out_specs=(P(None, ("dom", "rep"), None), P()),
        check_vma=False,
    )
```

```python
import jax
import jax.numpy as jnp
from jax import lax
from jax.experimental import pallas as pl
from jax.experimental.pallas import tpu as pltpu
from jax.sharding import PartitionSpec as P

MESH = pl.DeviceIdType.MESH
F32, BF16, I32 = jnp.float32, jnp.bfloat16, jnp.int32
VMEM = pl.BlockSpec(memory_space=pltpu.VMEM)
HBM = pl.BlockSpec(memory_space=pltpu.HBM)

NY, NZ, NC, NX = 4, 16, 2, 4
NYC = NY * NC
NDOM = NY * NZ * NC
D = 400
HALF = D // 2
RELS = 2000
RELPAD = 2048
SPAN = 1000
SLOTS = 1024
CHUNK = 1024
ROWS = 512
WIDE = 256
PIECES = ((0, 256), (256, 128), (384, 16))
NP = len(PIECES)
BACK = ((0, 256), (256, 144))
NB = len(BACK)
NH = 2
LANES = 128
XROWS = 112
XTILES = XROWS // 16
NEVER = -1e30


def nn(a, b):
    return lax.dot_general(a, b, (((1,), (0,)), ((), ())), preferred_element_type=F32)


def nt(a, b):
    return lax.dot_general(a, b, (((1,), (1,)), ((), ())), preferred_element_type=F32)


def tn(a, b):
    return lax.dot_general(a, b, (((0,), (0,)), ((), ())), preferred_element_type=F32)


def iota(shape, axis):
    return lax.broadcasted_iota(I32, shape, axis)


def onehot(hit):
    return jnp.where(hit, 1.0, 0.0).astype(BF16)


class Place:
    def __init__(self):
        dom, self.x = lax.axis_index("dom"), lax.axis_index("rep")
        self.c = lax.rem(dom, NC)
        self.z = lax.rem(lax.div(dom, NC), NZ)
        self.y = lax.div(dom, NC * NZ)
        self.yc = self.y * NC + self.c

    def at(self, z=None, y=None, yc=None, x=None):
        z = self.z if z is None else z
        x = self.x if x is None else x
        if y is not None:
            yc = y * NC + self.c
        yc = self.yc if yc is None else yc
        return {"dom": (lax.div(yc, NC) * NZ + z) * NC + lax.rem(yc, NC), "rep": x}

    def others(self, axis, body):
        size, me = {"z": (NZ, self.z), "yc": (NYC, self.yc), "x": (NX, self.x), "y": (NY, self.y)}[axis]

        def step(k, carry):
            away = size // 2 + lax.div(k, 2) * (1 - 2 * lax.rem(k, 2))
            body(lax.rem(me + away, size))
            return carry

        lax.fori_loop(1, size, step, 0)

    def greet(self, sem):
        def hello(**where):
            pl.semaphore_signal(sem, inc=1, device_id=self.at(**where), device_id_type=MESH)

        self.others("z", lambda p: hello(z=p))
        self.others("yc", lambda p: hello(yc=p))
        self.others("x", lambda p: hello(x=p))


def remote(src, dst, send, recv, where):
    return pltpu.make_async_remote_copy(
        src_ref=src, dst_ref=dst, send_sem=send, recv_sem=recv, device_id=where, device_id_type=MESH
    )


def arrived(group, sem):
    pltpu.make_async_copy(group, group, sem).wait()


SQUARE = (2 * NDOM, 2 * NDOM)


def bits(v, low, count):
    return lax.bitwise_and(lax.shift_right_logical(v, low), (1 << count) - 1)


def by_send_order():
    row, col = iota(SQUARE, 0), iota(SQUARE, 1)
    worker = (bits(row, 2, 2) * NZ + bits(row, 4, 4)) * NC + bits(row, 1, 1)
    return onehot(col == bits(row, 0, 1) * NDOM + worker)


def swap_zy():
    row, col = iota(SQUARE, 0), iota(SQUARE, 1)
    return onehot(col == bits(row, 1, 4) * 16 + bits(row, 5, 3) * 2 + bits(row, 0, 1))


def by_owner():
    row, col = iota(SQUARE, 0), iota(SQUARE, 1)
    owner = (bits(row, 6, 2) * NZ + bits(row, 1, 4)) * NC + bits(row, 5, 1)
    return onehot(col == bits(row, 0, 1) * NDOM + owner)


def kernel(
    count, ent_hbm, rel_hbm, head_hbm, relid_hbm, tail_hbm, neg_hbm, plan_hbm,
    ent_out, rel_out,
    stripe, rel, plan, raw, ids,
    snd1, rcv1, snd2, rcv2, gx,
    hb, tb, tr, logc, h1, t1, r1, ht, rt, tt, dr, dh, av, ql,
    es, rex, sb1, rb1, sb2, rb2,
    oc, rc, asend, aland, bsend, bland, zs, rz, agz, dback, fback, gback,
    s_in, s_1, r_1, s_2, r_2, s_3, r_3,
    s_e, r_e, s_b1, r_b1, s_b2, r_b2,
    s_c, r_c, s_a, r_a, s_b, r_b, s_z, r_z, s_az, r_az, s_d, r_d, s_f, r_f, s_g, r_g,
):
    me = Place()
    loads = [
        pltpu.make_async_copy(plan_hbm, plan, s_in.at[0]),
        pltpu.make_async_copy(ent_hbm.at[me.x], stripe, s_in.at[1]),
        pltpu.make_async_copy(head_hbm, raw.at[0], s_in.at[2]),
        pltpu.make_async_copy(relid_hbm, raw.at[1], s_in.at[3]),
        pltpu.make_async_copy(tail_hbm, raw.at[2], s_in.at[4]),
        pltpu.make_async_copy(neg_hbm, raw.at[3], s_in.at[5]),
        pltpu.make_async_copy(rel_hbm, rel, s_in.at[6]),
    ]
    for load in loads:
        load.start()
    hello = pltpu.get_barrier_semaphore()
    me.greet(hello)

    loads[0].wait()
    loads[1].wait()
    sq = (NDOM, NDOM)
    plan_hit = jnp.concatenate([onehot(iota(sq, 0) == plan[h : h + 1, :]) for h in range(2)], axis=1)
    picked = nn(stripe[...], plan_hit).astype(BF16)
    rows = nt(by_owner(), picked).astype(BF16)
    for p, (d, n) in enumerate(PIECES):
        snd2[p][...] = rows[:, d : d + n].reshape(NYC, 2 * NZ, n)

    def copy1(p, dst, src):
        return remote(snd1[p].at[dst], rcv1[p].at[src], s_1.at[p], r_1.at[p], me.at(z=dst))

    def copy2(p, dst, src):
        return remote(snd2[p].at[dst], rcv2[p].at[src], s_2.at[p], r_2.at[p], me.at(yc=dst))

    def copy3(p, dst, src):
        part = gx.at[src, pl.ds(*PIECES[p])]
        return remote(part, part, s_3, r_3.at[p], me.at(x=dst))
    pl.semaphore_wait(hello, NX + NYC + NZ - 3)
    for p in range(NP):
        me.others("yc", lambda q, p=p: copy2(p, q, me.yc).start())
        rcv2[p][me.yc] = snd2[p][me.yc]

    def over_z(p):
        arrived(rcv2[p].at[pl.ds(0, NYC - 1)], r_2.at[p])
        turned = tn(swap_zy(), rcv2[p][...].reshape(2 * NDOM, PIECES[p][1])).astype(BF16)
        snd1[p][...] = turned.reshape(NZ, 2 * NYC, PIECES[p][1])
        me.others("z", lambda q: copy1(p, q, me.z).start())
        rcv1[p][me.z] = snd1[p][me.z]

    def over_x(p):
        d, n = PIECES[p]
        arrived(rcv1[p].at[pl.ds(0, NZ - 1)], r_1.at[p])
        turned = tn(rcv1[p][...].reshape(2 * NDOM, n), by_send_order()).astype(BF16)
        gx[me.x, d : d + n] = turned
        me.others("x", lambda q: copy3(p, q, me.x).start())

    def relation_rows(k):
        at = slice(k * CHUNK, (k + 1) * CHUNK)
        r1[at, :] = onehot(iota((CHUNK, RELPAD), 1) == columns[at, 1:2])
        rt[:, at] = nt(rel[...], r1[at, 0:RELS]).astype(BF16)
    over_z(0)
    over_z(1)
    over_z(2)
    for load in loads[2:6]:
        load.wait()
    ids[...] = jnp.full(ids.shape, -4, I32)
    for k in range(4):
        ids[k : k + 1, 0:SPAN] = raw[k]
    given = ids[...]
    place = lax.bitwise_and(given, 3) * NDOM + lax.shift_right_arithmetic(given, 2)
    ids[...] = jnp.where(iota(ids.shape, 0) == 1, given, place)
    columns = ids[...].T
    loads[6].wait()
    for k in range(SLOTS // CHUNK):
        relation_rows(k)
    times = jnp.zeros((ROWS, 1), F32)
    for k in range(SLOTS // CHUNK):
        at = slice(k * CHUNK, (k + 1) * CHUNK)
        hit = iota((ROWS, CHUNK), 0) == ids[3:4, at]
        times += jnp.sum(jnp.where(hit, 1.0, 0.0), axis=1, keepdims=True)
        h1[:, at] = onehot(iota((ROWS, CHUNK), 0) == ids[0:1, at])
        t1[:, at] = onehot(iota((ROWS, CHUNK), 0) == ids[2:3, at])
    logc[...] = jnp.where(times > 0.0, jnp.log(jnp.maximum(times, 1.0)), NEVER)
    def rows_in(p):
        d, n = PIECES[p]
        arrived(gx.at[pl.ds(0, NX - 1), pl.ds(d, n)], r_3.at[p])
        for x in range(NX):
            lanes = slice(x * NDOM, (x + 1) * NDOM)
            hb[d : d + n, lanes] = gx[x, d : d + n, 0:NDOM]
            tb[d : d + n, lanes] = gx[x, d : d + n, NDOM:]
        tr[:, d : d + n] = tb[d : d + n, :].T
        ht[d : d + n, :] = nn(hb[d : d + n, :], h1[...]).astype(BF16)
        tt[d : d + n, :] = nn(tb[d : d + n, :], t1[...]).astype(BF16)
    over_x(0)
    over_x(1)
    over_x(2)
    rows_in(0)
    rows_in(1)
    rows_in(2)

    def chunk(k, carry):
        at = pl.ds(pl.multiple_of(k * CHUNK, CHUNK), CHUNK)
        h, r, t = ht[:, at].astype(F32), rt[:, at].astype(F32), tt[:, at].astype(F32)
        h_re, h_im = h[0:HALF], h[HALF:D]
        r_re, r_im = r[0:HALF], r[HALF:D]
        q_re = h_re * r_re - h_im * r_im
        q_im = h_re * r_im + h_im * r_re
        s0 = jnp.sum(q_re * t[0:HALF] + q_im * t[HALF:D], axis=0, keepdims=True)
        q_low = jnp.concatenate([q_re, q_im], axis=0).astype(BF16)
        ql[:, at] = q_low
        s = nn(tr[...], q_low) + logc[...]
        m = jnp.maximum(s0, jnp.max(s, axis=0, keepdims=True))
        e0 = jnp.exp(s0 - m)
        e = jnp.exp(s - m)
        z = e0 + jnp.sum(e, axis=0, keepdims=True)
        slot = iota((1, CHUNK), 1) + k * CHUNK
        valid = jnp.where(slot < count[0], 1.0, 0.0)
        g0 = valid * (e0 / z - 1.0)
        tail_hit = iota((ROWS, CHUNK), 0) == ids[2:3, at]
        a = (e * (valid / z) + jnp.where(tail_hit, g0, 0.0)).astype(BF16)
        av[:, at] = a
        dq = nn(tb[...], a)
        d_re, d_im = dq[0:HALF], dq[HALF:D]
        dh[:, at] = jnp.concatenate(
            [d_re * r_re + d_im * r_im, d_im * r_re - d_re * r_im], axis=0
        ).astype(BF16)
        dr[:, at] = jnp.concatenate(
            [d_re * h_re + d_im * h_im, d_im * h_re - d_re * h_im], axis=0
        ).astype(BF16)
        return carry
    lax.fori_loop(0, SLOTS // CHUNK, chunk, 0, unroll=True)

    def ent_copy(p, dst, src):
        part = pl.ds(*BACK[p])
        return remote(es.at[dst, part], rex.at[src, part], s_e, r_e.at[p], me.at(x=dst))

    def b1_copy(p, dst, src):
        return remote(sb1[p].at[dst], rb1[p].at[src], s_b1.at[p], r_b1.at[p], me.at(yc=dst))

    def b2_copy(p, dst, src):
        return remote(sb2[p].at[dst], rb2[p].at[src], s_b2.at[p], r_b2.at[p], me.at(z=dst))

    other_core = me.at(yc=me.y * NC + (1 - me.c))

    def core_copy(j):
        return remote(oc.at[j], rc.at[j], s_c, r_c.at[j], other_core)

    axes = (("y", "x"), ("x", "y"))
    index = {"x": me.x, "y": me.y}

    def copy_a(h, dst, src):
        return remote(asend.at[h, dst], aland.at[h, src], s_a.at[h], r_a.at[h], me.at(**{axes[h][0]: dst}))

    def copy_b(h, dst, src):
        return remote(bsend.at[h, dst], bland.at[h, src], s_b.at[h], r_b.at[h], me.at(**{axes[h][1]: dst}))

    def z_copy(dst, src):
        return remote(zs.at[dst], rz.at[src], s_z.at[dst], r_z, me.at(z=dst))

    def az_copy(dst, src):
        return remote(agz.at[src], agz.at[src], s_az, r_az.at[src], me.at(z=dst))

    def copy_d(h, dst, src):
        part = dback.at[h, src]
        return remote(part, part, s_d.at[h], r_d.at[h], me.at(**{axes[h][1]: dst}))

    def copy_f(h, dst, src):
        part = fback.at[h, src]
        return remote(part, part, s_f.at[h], r_f.at[h, src], me.at(**{axes[h][0]: dst}))

    def copy_g(h, j):
        return remote(fback.at[h, j], gback.at[h, j], s_g.at[h], r_g.at[h], other_core)

    def entity_block(x):
        lanes = pl.ds(pl.multiple_of(x * NDOM, NDOM), NDOM)
        es[x, :, 0:NDOM] = nt(dh[...], h1[lanes, :]).astype(BF16)
        es[x, :, NDOM : 2 * NDOM] = nt(ql[...], av[lanes, :]).astype(BF16)

    def entity_out(x):
        for p in range(NB):
            ent_copy(p, x, me.x).start()

    def relation_block(c, y):
        lanes = pl.ds(pl.multiple_of((c * NY + y) * WIDE, WIDE), WIDE)
        return nn(dr[...], r1[:, lanes])

    def to_core(j):
        oc[j] = relation_block(1 - me.c, j).astype(BF16)
        core_copy(j).start()

    def with_core(j):
        block = relation_block(me.c, j)
        core_copy(j).wait_recv()
        block = (block + rc[j].astype(F32)).astype(BF16)
        for h in range(NH):
            asend[h, j] = block[:, h * LANES : (h + 1) * LANES]

            @pl.when(j != index[axes[h][0]])
            def _(h=h):
                copy_a(h, j, index[axes[h][0]]).start()

    def each(body):
        def step(k, carry):
            body(lax.rem(me.y + k, NY))
            return carry

        lax.fori_loop(1, NY + 1, step, 0)

    def four(ref, h):
        return sum(ref[h, j].astype(F32) for j in range(NY))

    def rel_second(h):
        first, second = axes[h]
        aland[h, index[first]] = asend[h, index[first]]
        arrived(aland.at[h, pl.ds(0, NY - 1)], r_a.at[h])
        total = four(aland, h).astype(BF16)
        for j in range(NX):
            n = min(XROWS, D - j * XROWS)
            bsend[h, j, 0:n] = total[j * XROWS : j * XROWS + n]
            if n < XROWS:
                bsend[h, j, n:] = jnp.zeros((XROWS - n, LANES), BF16)
        me.others(second, lambda q: copy_b(h, q, index[second]).start())

    def tiles(body, parts=range(NH)):
        def step(i, carry):
            z = lax.div(i, XTILES) * 8 + lax.rem(i, XTILES)

            @pl.when(z != me.z)
            def _():
                body(z)

            return carry

        lax.fori_loop(parts[0] * XTILES, (parts[-1] + 1) * XTILES, step, 0)

    def rel_z(h):
        second = axes[h][1]
        bland[h, index[second]] = bsend[h, index[second]]
        arrived(bland.at[h, pl.ds(0, NX - 1)], r_b.at[h])
        zs[h * 8 : h * 8 + XTILES] = four(bland, h).astype(BF16).reshape(XTILES, 16, LANES)
        def to_owner(q):
            @pl.when(jnp.logical_and(lax.div(q, 8) == h, lax.rem(q, 8) < XTILES))
            def _():
                z_copy(q, me.z).start()

        me.others("z", to_owner)

    owns = lax.rem(me.z, 8) < XTILES

    def rel_az():
        @pl.when(owns)
        def _():
            rz[me.z] = zs[me.z]
            arrived(rz.at[pl.ds(0, NZ - 1)], r_z)
            total = rz[0].astype(F32)
            for z in range(1, NZ):
                total += rz[z].astype(F32)
            agz[me.z] = total.astype(BF16)
            me.others("z", lambda q: az_copy(q, me.z).start())

    def rel_back1(h):
        second = axes[h][1]
        tiles(lambda q: az_copy(q, q).wait_recv(), (h,))
        dback[h, index[second]] = agz[h * 8 : h * 8 + XTILES].reshape(XROWS, LANES)
        me.others(second, lambda q: copy_d(h, q, index[second]).start())

    def rel_back2(h):
        first = axes[h][0]
        arrived(dback.at[h, pl.ds(0, NX - 1)], r_d.at[h])
        for j in range(NX):
            n = min(XROWS, D - j * XROWS)
            fback[h, index[first], j * XROWS : j * XROWS + n] = dback[h, j, 0:n]
        me.others(first, lambda q: copy_f(h, q, index[first]).start())
        copy_g(h, index[first]).start()

    def rel_core():
        def step(k, carry):
            for h in range(NH):
                j = lax.rem(index[axes[h][0]] + k, NX)
                copy_f(h, j, j).wait_recv()
                copy_g(h, j).start()
            return carry

        lax.fori_loop(1, NX, step, 0)

    def rel_done():
        low = me.c == 0
        for h in range(NH):
            arrived(gback.at[h], r_g.at[h])
            for j in range(NY):
                here, there = fback[h, j].astype(F32), gback[h, j].astype(F32)
                for c in range(NC):
                    start = ((c * NY + j) * NH + h) * LANES
                    n = min(LANES, RELS - start)
                    block = jnp.where(low, here, there) if c == 0 else jnp.where(low, there, here)
                    rel_out[:, start : start + n] = block.astype(BF16)[:, 0:n]

    def ent_yc(p):
        d, n = BACK[p]
        rex[me.x, d : d + n] = es[me.x, d : d + n]
        arrived(rex.at[pl.ds(0, NX - 1), pl.ds(d, n)], r_e.at[p])
        total = sum(rex[x, d : d + n].astype(F32) for x in range(NX)).astype(BF16)
        turned = nt(by_owner(), total).astype(BF16).reshape(NYC, 2 * NZ, n)
        sb1[p][...] = turned
        me.others("yc", lambda q: b1_copy(p, q, me.yc).start())
        rb1[p][me.yc] = sb1[p][me.yc]

    def ent_rows(p):
        arrived(rb1[p].at[pl.ds(0, NYC - 1)], r_b1.at[p])
        turned = tn(swap_zy(), rb1[p][...].reshape(2 * NDOM, BACK[p][1])).astype(BF16)
        sb2[p][...] = turned.reshape(NZ, 2 * NYC, BACK[p][1])
        rb2[p][me.z] = sb2[p][me.z]

    def ent_z(p):
        me.others("z", lambda q: b2_copy(p, q, me.z).start())

    def ent_done(p, pick):
        d, n = BACK[p]
        arrived(rb2[p].at[pl.ds(0, NZ - 1)], r_b2.at[p])
        ent_out[d : d + n, :] = tn(rb2[p][...].reshape(2 * NDOM, n), pick).astype(BF16)
    each(to_core)
    each(with_core)
    me.others("x", entity_block)
    entity_block(me.x)
    parts = jnp.concatenate([onehot(iota(sq, 0) == plan[h : h + 1, :]) for h in range(2)], axis=1)
    pick = nt(by_send_order(), parts).astype(BF16)
    for h in range(NH):
        rel_second(h)
    me.others("x", entity_out)
    for h in range(NH):
        rel_z(h)
    for p in range(NB):
        ent_yc(p)
    rel_az()
    for p in range(NB):
        ent_rows(p)
    for h in range(NH):
        rel_back1(h)
    for p in range(NB):
        ent_z(p)
    for h in range(NH):
        rel_back2(h)
    rel_core()
    rel_done()
    for p in range(NB):
        ent_done(p, pick)
    arrived(gx.at[pl.ds(0, NX - 1)], s_3)
    arrived(es.at[pl.ds(0, NX - 1)], s_e)
    for p in range(NP):
        arrived(snd1[p].at[pl.ds(0, NZ - 1)], s_1.at[p])
        arrived(snd2[p].at[pl.ds(0, NYC - 1)], s_2.at[p])
    for p in range(NB):
        arrived(sb1[p].at[pl.ds(0, NYC - 1)], s_b1.at[p])
        arrived(sb2[p].at[pl.ds(0, NZ - 1)], s_b2.at[p])
    arrived(oc, s_c)
    for h in range(NH):
        arrived(asend.at[h, pl.ds(0, NY - 1)], s_a.at[h])
        arrived(bsend.at[h, pl.ds(0, NX - 1)], s_b.at[h])
        arrived(dback.at[h, pl.ds(0, NX - 1)], s_d.at[h])
        arrived(fback.at[h, pl.ds(0, NY - 1)], s_f.at[h])
        arrived(gback.at[h], s_g.at[h])
    tiles(lambda q: z_copy(q, me.z).wait_send())

    @pl.when(owns)
    def _():
        arrived(agz.at[pl.ds(0, NZ - 1)], s_az)


def scratch():
    def bf16(*shape):
        return pltpu.VMEM(shape, BF16)

    dma = pltpu.SemaphoreType.DMA

    def rows(pieces, *lead):
        return tuple(bf16(*lead, n) for _, n in pieces)

    by_z, by_yc = rows(PIECES, NZ, 2 * NYC), rows(PIECES, NYC, 2 * NZ)
    back_z, back_yc = rows(BACK, NZ, 2 * NYC), rows(BACK, NYC, 2 * NZ)
    block, slots, tile = bf16(NX, D, WIDE), bf16(D, SLOTS), bf16(NZ, 16, LANES)
    half, thin = bf16(NH, NY, D, LANES), bf16(NH, NX, XROWS, LANES)
    hops = [dma((NP,)), dma((NP,))]
    sides = [dma((NH,)), dma((NH,))]
    return (
        [bf16(D, NDOM), bf16(D, RELS), pltpu.VMEM((2, NDOM), I32)]
        + [pltpu.VMEM((4, 1, SPAN), I32), pltpu.VMEM((8, SLOTS), I32)]
        + [by_z, by_z, by_yc, by_yc, block]
        + [bf16(D, ROWS), bf16(D, ROWS), bf16(ROWS, D), pltpu.VMEM((ROWS, 1), F32)]
        + [bf16(ROWS, SLOTS), bf16(ROWS, SLOTS), bf16(SLOTS, RELPAD)]
        + [slots, slots, slots, slots, slots, bf16(ROWS, SLOTS), slots]
        + [block, block, back_yc, back_yc, back_z, back_z]
        + [block, block, half, half, thin, thin, tile, tile, tile, thin, half, half]
        + [dma((7,))]
        + hops * 2
        + [dma, dma((NP,)), dma, dma((NB,))]
        + [dma((NB,))] * 4
        + [dma, dma((NY,))]
        + sides * 2
        + [dma((NZ,)), dma, dma, dma((NZ,))]
        + sides
        + [dma((NH,)), dma((NH, NY))]
        + sides
    )


def per_device(entity, relation, head_ids, relation_ids, tail_ids, negative_ids, span_counts, plan):
    ent_out, rel_out = pl.pallas_call(
        kernel,
        out_shape=(
            jax.ShapeDtypeStruct((D, NDOM), BF16),
            jax.ShapeDtypeStruct((D, RELS), BF16),
        ),
        in_specs=[pl.BlockSpec(memory_space=pltpu.SMEM)] + [HBM] * 7,
        out_specs=(VMEM, VMEM),
        scratch_shapes=scratch(),
        compiler_params=pltpu.CompilerParams(
            collective_id=0, has_side_effects=True, vmem_limit_bytes=40 << 20
        ),
        name="bucket_round",
    )(
        span_counts,
        *(
            pltpu.with_memory_space_constraint(v, pltpu.HBM)
            for v in (
                jnp.transpose(entity, (1, 2, 0)),
                relation.T,
                head_ids.reshape(1, SPAN),
                relation_ids.reshape(1, SPAN),
                tail_ids.reshape(1, SPAN),
                negative_ids,
                plan.T,
            )
        ),
    )
    return jnp.transpose(ent_out.reshape(1, D, NDOM), (2, 0, 1)), rel_out.T


def solution(mesh):
    placed = (
        P(None, "dom", None),
        P(),
        P(("dom", "rep")),
        P(("dom", "rep")),
        P(("dom", "rep")),
        P(("dom", "rep"), None),
        P(("dom", "rep")),
        P(),
    )
    return jax.shard_map(
        per_device,
        mesh=mesh,
        in_specs=placed,
        out_specs=(P(None, ("dom", "rep"), None), P()),
        check_vma=False,
    )
```

```python
import jax
import jax.numpy as jnp
from jax import lax
from jax.experimental import pallas as pl
from jax.experimental.pallas import tpu as pltpu
from jax.sharding import PartitionSpec as P

MESH = pl.DeviceIdType.MESH
F32, BF16, I32 = jnp.float32, jnp.bfloat16, jnp.int32
VMEM = pl.BlockSpec(memory_space=pltpu.VMEM)
HBM = pl.BlockSpec(memory_space=pltpu.HBM)

NY, NZ, NC, NX = 4, 16, 2, 4
NYC = NY * NC
NDOM = NY * NZ * NC
D = 400
HALF = D // 2
RELS = 2000
RELPAD = 2048
SPAN = 1000
SLOTS = 1024
CHUNK = 1024
ROWS = 512
WIDE = 256
PIECES = ((0, 256), (256, 128), (384, 16))
NP = len(PIECES)
BACK = ((0, 256), (256, 144))
NB = len(BACK)
NH = 2
LANES = 128
XROWS = 112
XTILES = XROWS // 16
NEVER = -1e30


def nn(a, b):
    return lax.dot_general(a, b, (((1,), (0,)), ((), ())), preferred_element_type=F32)


def nt(a, b):
    return lax.dot_general(a, b, (((1,), (1,)), ((), ())), preferred_element_type=F32)


def tn(a, b):
    return lax.dot_general(a, b, (((0,), (0,)), ((), ())), preferred_element_type=F32)


def iota(shape, axis):
    return lax.broadcasted_iota(I32, shape, axis)


def onehot(hit):
    return jnp.where(hit, 1.0, 0.0).astype(BF16)


class Place:
    def __init__(self):
        dom, self.x = lax.axis_index("dom"), lax.axis_index("rep")
        self.c = lax.rem(dom, NC)
        self.z = lax.rem(lax.div(dom, NC), NZ)
        self.y = lax.div(dom, NC * NZ)
        self.yc = self.y * NC + self.c

    def at(self, z=None, y=None, yc=None, x=None):
        z = self.z if z is None else z
        x = self.x if x is None else x
        if y is not None:
            yc = y * NC + self.c
        yc = self.yc if yc is None else yc
        return {"dom": (lax.div(yc, NC) * NZ + z) * NC + lax.rem(yc, NC), "rep": x}

    def others(self, axis, body):
        size, me = {"z": (NZ, self.z), "yc": (NYC, self.yc), "x": (NX, self.x), "y": (NY, self.y)}[axis]

        def step(k, carry):
            away = size // 2 + lax.div(k, 2) * (1 - 2 * lax.rem(k, 2))
            body(lax.rem(me + away, size))
            return carry

        lax.fori_loop(1, size, step, 0)

    def greet(self, sem):
        def hello(**where):
            pl.semaphore_signal(sem, inc=1, device_id=self.at(**where), device_id_type=MESH)

        self.others("z", lambda p: hello(z=p))
        self.others("yc", lambda p: hello(yc=p))
        self.others("x", lambda p: hello(x=p))


def remote(src, dst, send, recv, where):
    return pltpu.make_async_remote_copy(
        src_ref=src, dst_ref=dst, send_sem=send, recv_sem=recv, device_id=where, device_id_type=MESH
    )


def arrived(group, sem):
    pltpu.make_async_copy(group, group, sem).wait()


SQUARE = (2 * NDOM, 2 * NDOM)


def bits(v, low, count):
    return lax.bitwise_and(lax.shift_right_logical(v, low), (1 << count) - 1)


def by_send_order():
    row, col = iota(SQUARE, 0), iota(SQUARE, 1)
    worker = (bits(row, 2, 2) * NZ + bits(row, 4, 4)) * NC + bits(row, 1, 1)
    return onehot(col == bits(row, 0, 1) * NDOM + worker)


def swap_zy():
    row, col = iota(SQUARE, 0), iota(SQUARE, 1)
    return onehot(col == bits(row, 1, 4) * 16 + bits(row, 5, 3) * 2 + bits(row, 0, 1))


def by_owner():
    row, col = iota(SQUARE, 0), iota(SQUARE, 1)
    owner = (bits(row, 6, 2) * NZ + bits(row, 1, 4)) * NC + bits(row, 5, 1)
    return onehot(col == bits(row, 0, 1) * NDOM + owner)


def kernel(
    count, ent_hbm, rel_hbm, head_hbm, relid_hbm, tail_hbm, neg_hbm, plan_hbm,
    ent_out, rel_out,
    stripe, rel, plan, raw, ids,
    snd1, rcv1, snd2, rcv2, gx,
    hb, tb, tr, logc, h1, t1, r1, ht, rt, tt, dr, dh, av, ql,
    es, rex, sb1, rb1, sb2, rb2,
    oc, rc, asend, aland, bsend, bland, zs, rz, agz, dback, fback, gback,
    s_in, s_1, r_1, s_2, r_2, s_3, r_3,
    s_e, r_e, s_b1, r_b1, s_b2, r_b2,
    s_c, r_c, s_a, r_a, s_b, r_b, s_z, r_z, s_az, r_az, s_d, r_d, s_f, r_f, s_g, r_g,
):
    me = Place()
    loads = [
        pltpu.make_async_copy(plan_hbm, plan, s_in.at[0]),
        pltpu.make_async_copy(ent_hbm.at[me.x], stripe, s_in.at[1]),
        pltpu.make_async_copy(head_hbm, raw.at[0], s_in.at[2]),
        pltpu.make_async_copy(relid_hbm, raw.at[1], s_in.at[3]),
        pltpu.make_async_copy(tail_hbm, raw.at[2], s_in.at[4]),
        pltpu.make_async_copy(neg_hbm, raw.at[3], s_in.at[5]),
        pltpu.make_async_copy(rel_hbm, rel, s_in.at[6]),
    ]
    hello = pltpu.get_barrier_semaphore()
    me.greet(hello)
    for load in loads:
        load.start()

    loads[0].wait()
    loads[1].wait()
    sq = (NDOM, NDOM)
    plan_hit = jnp.concatenate([onehot(iota(sq, 0) == plan[h : h + 1, :]) for h in range(2)], axis=1)
    picked = nn(stripe[...], plan_hit).astype(BF16)
    rows = nt(by_owner(), picked).astype(BF16)
    for p, (d, n) in enumerate(PIECES):
        snd2[p][...] = rows[:, d : d + n].reshape(NYC, 2 * NZ, n)

    def copy1(p, dst, src):
        return remote(snd1[p].at[dst], rcv1[p].at[src], s_1.at[p], r_1.at[p], me.at(z=dst))

    def copy2(p, dst, src):
        return remote(snd2[p].at[dst], rcv2[p].at[src], s_2.at[p], r_2.at[p], me.at(yc=dst))

    def copy3(p, dst, src):
        part = gx.at[src, pl.ds(*PIECES[p])]
        return remote(part, part, s_3, r_3.at[p], me.at(x=dst))
    pl.semaphore_wait(hello, NX + NYC + NZ - 3)
    for p in range(NP):
        me.others("yc", lambda q, p=p: copy2(p, q, me.yc).start())
        rcv2[p][me.yc] = snd2[p][me.yc]

    def over_z(p):
        arrived(rcv2[p].at[pl.ds(0, NYC - 1)], r_2.at[p])
        turned = tn(swap_zy(), rcv2[p][...].reshape(2 * NDOM, PIECES[p][1])).astype(BF16)
        snd1[p][...] = turned.reshape(NZ, 2 * NYC, PIECES[p][1])
        me.others("z", lambda q: copy1(p, q, me.z).start())
        rcv1[p][me.z] = snd1[p][me.z]

    def over_x(p):
        d, n = PIECES[p]
        arrived(rcv1[p].at[pl.ds(0, NZ - 1)], r_1.at[p])
        turned = tn(rcv1[p][...].reshape(2 * NDOM, n), by_send_order()).astype(BF16)
        gx[me.x, d : d + n] = turned
        me.others("x", lambda q: copy3(p, q, me.x).start())

    def relation_rows(k):
        at = slice(k * CHUNK, (k + 1) * CHUNK)
        r1[at, :] = onehot(iota((CHUNK, RELPAD), 1) == columns[at, 1:2])
        rt[:, at] = nt(rel[...], r1[at, 0:RELS]).astype(BF16)
    over_z(0)
    over_z(1)
    over_z(2)
    for load in loads[2:6]:
        load.wait()
    ids[...] = jnp.full(ids.shape, -4, I32)
    for k in range(4):
        ids[k : k + 1, 0:SPAN] = raw[k]
    given = ids[...]
    place = lax.bitwise_and(given, 3) * NDOM + lax.shift_right_arithmetic(given, 2)
    ids[...] = jnp.where(iota(ids.shape, 0) == 1, given, place)
    columns = ids[...].T
    loads[6].wait()
    for k in range(SLOTS // CHUNK):
        relation_rows(k)
    times = jnp.zeros((ROWS, 1), F32)
    for k in range(SLOTS // CHUNK):
        at = slice(k * CHUNK, (k + 1) * CHUNK)
        hit = iota((ROWS, CHUNK), 0) == ids[3:4, at]
        times += jnp.sum(jnp.where(hit, 1.0, 0.0), axis=1, keepdims=True)
        h1[:, at] = onehot(iota((ROWS, CHUNK), 0) == ids[0:1, at])
        t1[:, at] = onehot(iota((ROWS, CHUNK), 0) == ids[2:3, at])
    logc[...] = jnp.where(times > 0.0, jnp.log(jnp.maximum(times, 1.0)), NEVER)
    def rows_in(p):
        d, n = PIECES[p]
        arrived(gx.at[pl.ds(0, NX - 1), pl.ds(d, n)], r_3.at[p])
        for x in range(NX):
            lanes = slice(x * NDOM, (x + 1) * NDOM)
            hb[d : d + n, lanes] = gx[x, d : d + n, 0:NDOM]
            tb[d : d + n, lanes] = gx[x, d : d + n, NDOM:]
        tr[:, d : d + n] = tb[d : d + n, :].T
        ht[d : d + n, :] = nn(hb[d : d + n, :], h1[...]).astype(BF16)
        tt[d : d + n, :] = nn(tb[d : d + n, :], t1[...]).astype(BF16)
    over_x(0)
    over_x(1)
    over_x(2)
    rows_in(0)
    rows_in(1)
    rows_in(2)

    def chunk(k, carry):
        at = pl.ds(pl.multiple_of(k * CHUNK, CHUNK), CHUNK)
        h, r, t = ht[:, at].astype(F32), rt[:, at].astype(F32), tt[:, at].astype(F32)
        h_re, h_im = h[0:HALF], h[HALF:D]
        r_re, r_im = r[0:HALF], r[HALF:D]
        q_re = h_re * r_re - h_im * r_im
        q_im = h_re * r_im + h_im * r_re
        s0 = jnp.sum(q_re * t[0:HALF] + q_im * t[HALF:D], axis=0, keepdims=True)
        q_low = jnp.concatenate([q_re, q_im], axis=0).astype(BF16)
        ql[:, at] = q_low
        s = nn(tr[...], q_low) + logc[...]
        m = jnp.maximum(s0, jnp.max(s, axis=0, keepdims=True))
        e0 = jnp.exp(s0 - m)
        e = jnp.exp(s - m)
        z = e0 + jnp.sum(e, axis=0, keepdims=True)
        slot = iota((1, CHUNK), 1) + k * CHUNK
        valid = jnp.where(slot < count[0], 1.0, 0.0)
        g0 = valid * (e0 / z - 1.0)
        tail_hit = iota((ROWS, CHUNK), 0) == ids[2:3, at]
        a = (e * (valid / z) + jnp.where(tail_hit, g0, 0.0)).astype(BF16)
        av[:, at] = a
        dq = nn(tb[...], a)
        d_re, d_im = dq[0:HALF], dq[HALF:D]
        dh[:, at] = jnp.concatenate(
            [d_re * r_re + d_im * r_im, d_im * r_re - d_re * r_im], axis=0
        ).astype(BF16)
        dr[:, at] = jnp.concatenate(
            [d_re * h_re + d_im * h_im, d_im * h_re - d_re * h_im], axis=0
        ).astype(BF16)
        return carry
    lax.fori_loop(0, SLOTS // CHUNK, chunk, 0, unroll=True)

    def ent_copy(p, dst, src):
        part = pl.ds(*BACK[p])
        return remote(es.at[dst, part], rex.at[src, part], s_e, r_e.at[p], me.at(x=dst))

    def b1_copy(p, dst, src):
        return remote(sb1[p].at[dst], rb1[p].at[src], s_b1.at[p], r_b1.at[p], me.at(yc=dst))

    def b2_copy(p, dst, src):
        return remote(sb2[p].at[dst], rb2[p].at[src], s_b2.at[p], r_b2.at[p], me.at(z=dst))

    other_core = me.at(yc=me.y * NC + (1 - me.c))

    def core_copy(j):
        return remote(oc.at[j], rc.at[j], s_c, r_c.at[j], other_core)

    axes = (("y", "x"), ("x", "y"))
    index = {"x": me.x, "y": me.y}

    def copy_a(h, dst, src):
        return remote(asend.at[h, dst], aland.at[h, src], s_a.at[h], r_a.at[h], me.at(**{axes[h][0]: dst}))

    def copy_b(h, dst, src):
        return remote(bsend.at[h, dst], bland.at[h, src], s_b.at[h], r_b.at[h], me.at(**{axes[h][1]: dst}))

    def z_copy(dst, src):
        return remote(zs.at[dst], rz.at[src], s_z.at[dst], r_z, me.at(z=dst))

    def az_copy(dst, src):
        return remote(agz.at[src], agz.at[src], s_az, r_az.at[src], me.at(z=dst))

    def copy_d(h, dst, src):
        part = dback.at[h, src]
        return remote(part, part, s_d.at[h], r_d.at[h], me.at(**{axes[h][1]: dst}))

    def copy_f(h, dst, src):
        part = fback.at[h, src]
        return remote(part, part, s_f.at[h], r_f.at[h, src], me.at(**{axes[h][0]: dst}))

    def copy_g(h, j):
        return remote(fback.at[h, j], gback.at[h, j], s_g.at[h], r_g.at[h], other_core)

    def entity_block(x):
        lanes = pl.ds(pl.multiple_of(x * NDOM, NDOM), NDOM)
        es[x, :, 0:NDOM] = nt(dh[...], h1[lanes, :]).astype(BF16)
        es[x, :, NDOM : 2 * NDOM] = nt(ql[...], av[lanes, :]).astype(BF16)

    def entity_out(x):
        for p in range(NB):
            ent_copy(p, x, me.x).start()

    def relation_block(c, y):
        lanes = pl.ds(pl.multiple_of((c * NY + y) * WIDE, WIDE), WIDE)
        return nn(dr[...], r1[:, lanes])

    def to_core(j):
        oc[j] = relation_block(1 - me.c, j).astype(BF16)
        core_copy(j).start()

    def with_core(j):
        block = relation_block(me.c, j)
        core_copy(j).wait_recv()
        block = (block + rc[j].astype(F32)).astype(BF16)
        for h in range(NH):
            asend[h, j] = block[:, h * LANES : (h + 1) * LANES]

            @pl.when(j != index[axes[h][0]])
            def _(h=h):
                copy_a(h, j, index[axes[h][0]]).start()

    def each(body):
        def step(k, carry):
            body(lax.rem(me.y + k, NY))
            return carry

        lax.fori_loop(1, NY + 1, step, 0)

    def four(ref, h):
        return sum(ref[h, j].astype(F32) for j in range(NY))

    def rel_second(h):
        first, second = axes[h]
        aland[h, index[first]] = asend[h, index[first]]
        arrived(aland.at[h, pl.ds(0, NY - 1)], r_a.at[h])
        total = four(aland, h).astype(BF16)
        for j in range(NX):
            n = min(XROWS, D - j * XROWS)
            bsend[h, j, 0:n] = total[j * XROWS : j * XROWS + n]
            if n < XROWS:
                bsend[h, j, n:] = jnp.zeros((XROWS - n, LANES), BF16)
        me.others(second, lambda q: copy_b(h, q, index[second]).start())

    def tiles(body, parts=range(NH)):
        def step(i, carry):
            z = lax.div(i, XTILES) * 8 + lax.rem(i, XTILES)

            @pl.when(z != me.z)
            def _():
                body(z)

            return carry

        lax.fori_loop(parts[0] * XTILES, (parts[-1] + 1) * XTILES, step, 0)

    def rel_z(h):
        second = axes[h][1]
        bland[h, index[second]] = bsend[h, index[second]]
        arrived(bland.at[h, pl.ds(0, NX - 1)], r_b.at[h])
        zs[h * 8 : h * 8 + XTILES] = four(bland, h).astype(BF16).reshape(XTILES, 16, LANES)
        def to_owner(q):
            @pl.when(jnp.logical_and(lax.div(q, 8) == h, lax.rem(q, 8) < XTILES))
            def _():
                z_copy(q, me.z).start()

        me.others("z", to_owner)

    owns = lax.rem(me.z, 8) < XTILES

    def rel_az():
        @pl.when(owns)
        def _():
            rz[me.z] = zs[me.z]
            arrived(rz.at[pl.ds(0, NZ - 1)], r_z)
            total = rz[0].astype(F32)
            for z in range(1, NZ):
                total += rz[z].astype(F32)
            agz[me.z] = total.astype(BF16)
            me.others("z", lambda q: az_copy(q, me.z).start())

    def rel_back1(h):
        second = axes[h][1]
        tiles(lambda q: az_copy(q, q).wait_recv(), (h,))
        dback[h, index[second]] = agz[h * 8 : h * 8 + XTILES].reshape(XROWS, LANES)
        me.others(second, lambda q: copy_d(h, q, index[second]).start())

    def rel_back2(h):
        first = axes[h][0]
        arrived(dback.at[h, pl.ds(0, NX - 1)], r_d.at[h])
        for j in range(NX):
            n = min(XROWS, D - j * XROWS)
            fback[h, index[first], j * XROWS : j * XROWS + n] = dback[h, j, 0:n]
        me.others(first, lambda q: copy_f(h, q, index[first]).start())
        copy_g(h, index[first]).start()

    def rel_core():
        def step(k, carry):
            for h in range(NH):
                j = lax.rem(index[axes[h][0]] + k, NX)
                copy_f(h, j, j).wait_recv()
                copy_g(h, j).start()
            return carry

        lax.fori_loop(1, NX, step, 0)

    def rel_done():
        low = me.c == 0
        for h in range(NH):
            arrived(gback.at[h], r_g.at[h])
            for j in range(NY):
                here, there = fback[h, j].astype(F32), gback[h, j].astype(F32)
                for c in range(NC):
                    start = ((c * NY + j) * NH + h) * LANES
                    n = min(LANES, RELS - start)
                    block = jnp.where(low, here, there) if c == 0 else jnp.where(low, there, here)
                    rel_out[:, start : start + n] = block.astype(BF16)[:, 0:n]

    def ent_yc(p):
        d, n = BACK[p]
        rex[me.x, d : d + n] = es[me.x, d : d + n]
        arrived(rex.at[pl.ds(0, NX - 1), pl.ds(d, n)], r_e.at[p])
        total = sum(rex[x, d : d + n].astype(F32) for x in range(NX)).astype(BF16)
        turned = nt(by_owner(), total).astype(BF16).reshape(NYC, 2 * NZ, n)
        sb1[p][...] = turned
        me.others("yc", lambda q: b1_copy(p, q, me.yc).start())
        rb1[p][me.yc] = sb1[p][me.yc]

    def ent_rows(p):
        arrived(rb1[p].at[pl.ds(0, NYC - 1)], r_b1.at[p])
        turned = tn(swap_zy(), rb1[p][...].reshape(2 * NDOM, BACK[p][1])).astype(BF16)
        sb2[p][...] = turned.reshape(NZ, 2 * NYC, BACK[p][1])
        rb2[p][me.z] = sb2[p][me.z]

    def ent_z(p):
        me.others("z", lambda q: b2_copy(p, q, me.z).start())

    def ent_done(p, pick):
        d, n = BACK[p]
        arrived(rb2[p].at[pl.ds(0, NZ - 1)], r_b2.at[p])
        ent_out[d : d + n, :] = tn(rb2[p][...].reshape(2 * NDOM, n), pick).astype(BF16)
    each(to_core)
    each(with_core)
    me.others("x", entity_block)
    entity_block(me.x)
    parts = jnp.concatenate([onehot(iota(sq, 0) == plan[h : h + 1, :]) for h in range(2)], axis=1)
    pick = nt(by_send_order(), parts).astype(BF16)
    rel_second(0)
    me.others("x", entity_out)
    rel_second(1)
    for h in range(NH):
        rel_z(h)
    for p in range(NB):
        ent_yc(p)
    rel_az()
    for p in range(NB):
        ent_rows(p)
    for h in range(NH):
        rel_back1(h)
    for p in range(NB):
        ent_z(p)
    for h in range(NH):
        rel_back2(h)
    rel_core()
    rel_done()
    for p in range(NB):
        ent_done(p, pick)
    arrived(gx.at[pl.ds(0, NX - 1)], s_3)
    arrived(es.at[pl.ds(0, NX - 1)], s_e)
    for p in range(NP):
        arrived(snd1[p].at[pl.ds(0, NZ - 1)], s_1.at[p])
        arrived(snd2[p].at[pl.ds(0, NYC - 1)], s_2.at[p])
    for p in range(NB):
        arrived(sb1[p].at[pl.ds(0, NYC - 1)], s_b1.at[p])
        arrived(sb2[p].at[pl.ds(0, NZ - 1)], s_b2.at[p])
    arrived(oc, s_c)
    for h in range(NH):
        arrived(asend.at[h, pl.ds(0, NY - 1)], s_a.at[h])
        arrived(bsend.at[h, pl.ds(0, NX - 1)], s_b.at[h])
        arrived(dback.at[h, pl.ds(0, NX - 1)], s_d.at[h])
        arrived(fback.at[h, pl.ds(0, NY - 1)], s_f.at[h])
        arrived(gback.at[h], s_g.at[h])
    tiles(lambda q: z_copy(q, me.z).wait_send())

    @pl.when(owns)
    def _():
        arrived(agz.at[pl.ds(0, NZ - 1)], s_az)


def scratch():
    def bf16(*shape):
        return pltpu.VMEM(shape, BF16)

    dma = pltpu.SemaphoreType.DMA

    def rows(pieces, *lead):
        return tuple(bf16(*lead, n) for _, n in pieces)

    by_z, by_yc = rows(PIECES, NZ, 2 * NYC), rows(PIECES, NYC, 2 * NZ)
    back_z, back_yc = rows(BACK, NZ, 2 * NYC), rows(BACK, NYC, 2 * NZ)
    block, slots, tile = bf16(NX, D, WIDE), bf16(D, SLOTS), bf16(NZ, 16, LANES)
    half, thin = bf16(NH, NY, D, LANES), bf16(NH, NX, XROWS, LANES)
    hops = [dma((NP,)), dma((NP,))]
    sides = [dma((NH,)), dma((NH,))]
    return (
        [bf16(D, NDOM), bf16(D, RELS), pltpu.VMEM((2, NDOM), I32)]
        + [pltpu.VMEM((4, 1, SPAN), I32), pltpu.VMEM((8, SLOTS), I32)]
        + [by_z, by_z, by_yc, by_yc, block]
        + [bf16(D, ROWS), bf16(D, ROWS), bf16(ROWS, D), pltpu.VMEM((ROWS, 1), F32)]
        + [bf16(ROWS, SLOTS), bf16(ROWS, SLOTS), bf16(SLOTS, RELPAD)]
        + [slots, slots, slots, slots, slots, bf16(ROWS, SLOTS), slots]
        + [block, block, back_yc, back_yc, back_z, back_z]
        + [block, block, half, half, thin, thin, tile, tile, tile, thin, half, half]
        + [dma((7,))]
        + hops * 2
        + [dma, dma((NP,)), dma, dma((NB,))]
        + [dma((NB,))] * 4
        + [dma, dma((NY,))]
        + sides * 2
        + [dma((NZ,)), dma, dma, dma((NZ,))]
        + sides
        + [dma((NH,)), dma((NH, NY))]
        + sides
    )


def per_device(entity, relation, head_ids, relation_ids, tail_ids, negative_ids, span_counts, plan):
    ent_out, rel_out = pl.pallas_call(
        kernel,
        out_shape=(
            jax.ShapeDtypeStruct((D, NDOM), BF16),
            jax.ShapeDtypeStruct((D, RELS), BF16),
        ),
        in_specs=[pl.BlockSpec(memory_space=pltpu.SMEM)] + [HBM] * 7,
        out_specs=(VMEM, VMEM),
        scratch_shapes=scratch(),
        compiler_params=pltpu.CompilerParams(
            collective_id=0, has_side_effects=True, vmem_limit_bytes=40 << 20
        ),
        name="bucket_round",
    )(
        span_counts,
        *(
            pltpu.with_memory_space_constraint(v, pltpu.HBM)
            for v in (
                jnp.transpose(entity, (1, 2, 0)),
                relation.T,
                head_ids.reshape(1, SPAN),
                relation_ids.reshape(1, SPAN),
                tail_ids.reshape(1, SPAN),
                negative_ids,
                plan.T,
            )
        ),
    )
    return jnp.transpose(ent_out.reshape(1, D, NDOM), (2, 0, 1)), rel_out.T


def solution(mesh):
    placed = (
        P(None, "dom", None),
        P(),
        P(("dom", "rep")),
        P(("dom", "rep")),
        P(("dom", "rep")),
        P(("dom", "rep"), None),
        P(("dom", "rep")),
        P(),
    )
    return jax.shard_map(
        per_device,
        mesh=mesh,
        in_specs=placed,
        out_specs=(P(None, ("dom", "rep"), None), P()),
        check_vma=False,
    )
```

```python
import jax
import jax.numpy as jnp
from jax import lax
from jax.experimental import pallas as pl
from jax.experimental.pallas import tpu as pltpu
from jax.sharding import PartitionSpec as P

MESH = pl.DeviceIdType.MESH
F32, BF16, I32 = jnp.float32, jnp.bfloat16, jnp.int32
VMEM = pl.BlockSpec(memory_space=pltpu.VMEM)
HBM = pl.BlockSpec(memory_space=pltpu.HBM)

NY, NZ, NC, NX = 4, 16, 2, 4
NYC = NY * NC
NDOM = NY * NZ * NC
D = 400
HALF = D // 2
RELS = 2000
RELPAD = 2048
SPAN = 1000
SLOTS = 1024
CHUNK = 1024
ROWS = 512
WIDE = 256
PIECES = ((0, 256), (256, 128), (384, 16))
NP = len(PIECES)
BACK = ((0, 400),)
NB = len(BACK)
NH = 2
LANES = 128
XROWS = 112
XTILES = XROWS // 16
NEVER = -1e30


def nn(a, b):
    return lax.dot_general(a, b, (((1,), (0,)), ((), ())), preferred_element_type=F32)


def nt(a, b):
    return lax.dot_general(a, b, (((1,), (1,)), ((), ())), preferred_element_type=F32)


def tn(a, b):
    return lax.dot_general(a, b, (((0,), (0,)), ((), ())), preferred_element_type=F32)


def iota(shape, axis):
    return lax.broadcasted_iota(I32, shape, axis)


def onehot(hit):
    return jnp.where(hit, 1.0, 0.0).astype(BF16)


class Place:
    def __init__(self):
        dom, self.x = lax.axis_index("dom"), lax.axis_index("rep")
        self.c = lax.rem(dom, NC)
        self.z = lax.rem(lax.div(dom, NC), NZ)
        self.y = lax.div(dom, NC * NZ)
        self.yc = self.y * NC + self.c

    def at(self, z=None, y=None, yc=None, x=None):
        z = self.z if z is None else z
        x = self.x if x is None else x
        if y is not None:
            yc = y * NC + self.c
        yc = self.yc if yc is None else yc
        return {"dom": (lax.div(yc, NC) * NZ + z) * NC + lax.rem(yc, NC), "rep": x}

    def others(self, axis, body):
        size, me = {"z": (NZ, self.z), "yc": (NYC, self.yc), "x": (NX, self.x), "y": (NY, self.y)}[axis]

        def step(k, carry):
            away = size // 2 + lax.div(k, 2) * (1 - 2 * lax.rem(k, 2))
            body(lax.rem(me + away, size))
            return carry

        lax.fori_loop(1, size, step, 0)

    def greet(self, sem):
        def hello(**where):
            pl.semaphore_signal(sem, inc=1, device_id=self.at(**where), device_id_type=MESH)

        self.others("z", lambda p: hello(z=p))
        self.others("yc", lambda p: hello(yc=p))
        self.others("x", lambda p: hello(x=p))


def remote(src, dst, send, recv, where):
    return pltpu.make_async_remote_copy(
        src_ref=src, dst_ref=dst, send_sem=send, recv_sem=recv, device_id=where, device_id_type=MESH
    )


def arrived(group, sem):
    pltpu.make_async_copy(group, group, sem).wait()


SQUARE = (2 * NDOM, 2 * NDOM)


def bits(v, low, count):
    return lax.bitwise_and(lax.shift_right_logical(v, low), (1 << count) - 1)


def by_send_order():
    row, col = iota(SQUARE, 0), iota(SQUARE, 1)
    worker = (bits(row, 2, 2) * NZ + bits(row, 4, 4)) * NC + bits(row, 1, 1)
    return onehot(col == bits(row, 0, 1) * NDOM + worker)


def swap_zy():
    row, col = iota(SQUARE, 0), iota(SQUARE, 1)
    return onehot(col == bits(row, 1, 4) * 16 + bits(row, 5, 3) * 2 + bits(row, 0, 1))


def by_owner():
    row, col = iota(SQUARE, 0), iota(SQUARE, 1)
    owner = (bits(row, 6, 2) * NZ + bits(row, 1, 4)) * NC + bits(row, 5, 1)
    return onehot(col == bits(row, 0, 1) * NDOM + owner)


def kernel(
    count, ent_hbm, rel_hbm, head_hbm, relid_hbm, tail_hbm, neg_hbm, plan_hbm,
    ent_out, rel_out,
    stripe, rel, plan, raw, ids,
    snd1, rcv1, snd2, rcv2, gx,
    hb, tb, tr, logc, h1, t1, r1, ht, rt, tt, dr, dh, av, ql,
    es, rex, sb1, rb1, sb2, rb2,
    oc, rc, asend, aland, bsend, bland, zs, rz, agz, dback, fback, gback,
    s_in, s_1, r_1, s_2, r_2, s_3, r_3,
    s_e, r_e, s_b1, r_b1, s_b2, r_b2,
    s_c, r_c, s_a, r_a, s_b, r_b, s_z, r_z, s_az, r_az, s_d, r_d, s_f, r_f, s_g, r_g,
):
    me = Place()
    loads = [
        pltpu.make_async_copy(plan_hbm, plan, s_in.at[0]),
        pltpu.make_async_copy(ent_hbm.at[me.x], stripe, s_in.at[1]),
        pltpu.make_async_copy(head_hbm, raw.at[0], s_in.at[2]),
        pltpu.make_async_copy(relid_hbm, raw.at[1], s_in.at[3]),
        pltpu.make_async_copy(tail_hbm, raw.at[2], s_in.at[4]),
        pltpu.make_async_copy(neg_hbm, raw.at[3], s_in.at[5]),
        pltpu.make_async_copy(rel_hbm, rel, s_in.at[6]),
    ]
    hello = pltpu.get_barrier_semaphore()
    me.greet(hello)
    for load in loads:
        load.start()

    loads[0].wait()
    loads[1].wait()
    sq = (NDOM, NDOM)
    plan_hit = jnp.concatenate([onehot(iota(sq, 0) == plan[h : h + 1, :]) for h in range(2)], axis=1)
    picked = nn(stripe[...], plan_hit).astype(BF16)
    rows = nt(by_owner(), picked).astype(BF16)
    for p, (d, n) in enumerate(PIECES):
        snd2[p][...] = rows[:, d : d + n].reshape(NYC, 2 * NZ, n)

    def copy1(p, dst, src):
        return remote(snd1[p].at[dst], rcv1[p].at[src], s_1.at[p], r_1.at[p], me.at(z=dst))

    def copy2(p, dst, src):
        return remote(snd2[p].at[dst], rcv2[p].at[src], s_2.at[p], r_2.at[p], me.at(yc=dst))

    def copy3(p, dst, src):
        part = gx.at[src, pl.ds(*PIECES[p])]
        return remote(part, part, s_3, r_3.at[p], me.at(x=dst))
    pl.semaphore_wait(hello, NX + NYC + NZ - 3)
    for p in range(NP):
        me.others("yc", lambda q, p=p: copy2(p, q, me.yc).start())
        rcv2[p][me.yc] = snd2[p][me.yc]

    def over_z(p):
        arrived(rcv2[p].at[pl.ds(0, NYC - 1)], r_2.at[p])
        turned = tn(swap_zy(), rcv2[p][...].reshape(2 * NDOM, PIECES[p][1])).astype(BF16)
        snd1[p][...] = turned.reshape(NZ, 2 * NYC, PIECES[p][1])
        me.others("z", lambda q: copy1(p, q, me.z).start())
        rcv1[p][me.z] = snd1[p][me.z]

    def over_x(p):
        d, n = PIECES[p]
        arrived(rcv1[p].at[pl.ds(0, NZ - 1)], r_1.at[p])
        turned = tn(rcv1[p][...].reshape(2 * NDOM, n), by_send_order()).astype(BF16)
        gx[me.x, d : d + n] = turned
        me.others("x", lambda q: copy3(p, q, me.x).start())

    def relation_rows(k):
        at = slice(k * CHUNK, (k + 1) * CHUNK)
        r1[at, :] = onehot(iota((CHUNK, RELPAD), 1) == columns[at, 1:2])
        rt[:, at] = nt(rel[...], r1[at, 0:RELS]).astype(BF16)
    over_z(0)
    over_z(1)
    over_z(2)
    for load in loads[2:6]:
        load.wait()
    ids[...] = jnp.full(ids.shape, -4, I32)
    for k in range(4):
        ids[k : k + 1, 0:SPAN] = raw[k]
    given = ids[...]
    place = lax.bitwise_and(given, 3) * NDOM + lax.shift_right_arithmetic(given, 2)
    ids[...] = jnp.where(iota(ids.shape, 0) == 1, given, place)
    columns = ids[...].T
    loads[6].wait()
    for k in range(SLOTS // CHUNK):
        relation_rows(k)
    times = jnp.zeros((ROWS, 1), F32)
    for k in range(SLOTS // CHUNK):
        at = slice(k * CHUNK, (k + 1) * CHUNK)
        hit = iota((ROWS, CHUNK), 0) == ids[3:4, at]
        times += jnp.sum(jnp.where(hit, 1.0, 0.0), axis=1, keepdims=True)
        h1[:, at] = onehot(iota((ROWS, CHUNK), 0) == ids[0:1, at])
        t1[:, at] = onehot(iota((ROWS, CHUNK), 0) == ids[2:3, at])
    logc[...] = jnp.where(times > 0.0, jnp.log(jnp.maximum(times, 1.0)), NEVER)
    def rows_in(p):
        d, n = PIECES[p]
        arrived(gx.at[pl.ds(0, NX - 1), pl.ds(d, n)], r_3.at[p])
        for x in range(NX):
            lanes = slice(x * NDOM, (x + 1) * NDOM)
            hb[d : d + n, lanes] = gx[x, d : d + n, 0:NDOM]
            tb[d : d + n, lanes] = gx[x, d : d + n, NDOM:]
        tr[:, d : d + n] = tb[d : d + n, :].T
        ht[d : d + n, :] = nn(hb[d : d + n, :], h1[...]).astype(BF16)
        tt[d : d + n, :] = nn(tb[d : d + n, :], t1[...]).astype(BF16)
    over_x(0)
    over_x(1)
    over_x(2)
    rows_in(0)
    rows_in(1)
    rows_in(2)

    def chunk(k, carry):
        at = pl.ds(pl.multiple_of(k * CHUNK, CHUNK), CHUNK)
        h, r, t = ht[:, at].astype(F32), rt[:, at].astype(F32), tt[:, at].astype(F32)
        h_re, h_im = h[0:HALF], h[HALF:D]
        r_re, r_im = r[0:HALF], r[HALF:D]
        q_re = h_re * r_re - h_im * r_im
        q_im = h_re * r_im + h_im * r_re
        s0 = jnp.sum(q_re * t[0:HALF] + q_im * t[HALF:D], axis=0, keepdims=True)
        q_low = jnp.concatenate([q_re, q_im], axis=0).astype(BF16)
        ql[:, at] = q_low
        s = nn(tr[...], q_low) + logc[...]
        m = jnp.maximum(s0, jnp.max(s, axis=0, keepdims=True))
        e0 = jnp.exp(s0 - m)
        e = jnp.exp(s - m)
        z = e0 + jnp.sum(e, axis=0, keepdims=True)
        slot = iota((1, CHUNK), 1) + k * CHUNK
        valid = jnp.where(slot < count[0], 1.0, 0.0)
        g0 = valid * (e0 / z - 1.0)
        tail_hit = iota((ROWS, CHUNK), 0) == ids[2:3, at]
        a = (e * (valid / z) + jnp.where(tail_hit, g0, 0.0)).astype(BF16)
        av[:, at] = a
        dq = nn(tb[...], a)
        d_re, d_im = dq[0:HALF], dq[HALF:D]
        dh[:, at] = jnp.concatenate(
            [d_re * r_re + d_im * r_im, d_im * r_re - d_re * r_im], axis=0
        ).astype(BF16)
        dr[:, at] = jnp.concatenate(
            [d_re * h_re + d_im * h_im, d_im * h_re - d_re * h_im], axis=0
        ).astype(BF16)
        return carry
    lax.fori_loop(0, SLOTS // CHUNK, chunk, 0, unroll=True)

    def ent_copy(p, dst, src):
        part = pl.ds(*BACK[p])
        return remote(es.at[dst, part], rex.at[src, part], s_e, r_e.at[p], me.at(x=dst))

    def b1_copy(p, dst, src):
        return remote(sb1[p].at[dst], rb1[p].at[src], s_b1.at[p], r_b1.at[p], me.at(yc=dst))

    def b2_copy(p, dst, src):
        return remote(sb2[p].at[dst], rb2[p].at[src], s_b2.at[p], r_b2.at[p], me.at(z=dst))

    other_core = me.at(yc=me.y * NC + (1 - me.c))

    def core_copy(j):
        return remote(oc.at[j], rc.at[j], s_c, r_c.at[j], other_core)

    axes = (("y", "x"), ("x", "y"))
    index = {"x": me.x, "y": me.y}

    def copy_a(h, dst, src):
        return remote(asend.at[h, dst], aland.at[h, src], s_a.at[h], r_a.at[h], me.at(**{axes[h][0]: dst}))

    def copy_b(h, dst, src):
        return remote(bsend.at[h, dst], bland.at[h, src], s_b.at[h], r_b.at[h], me.at(**{axes[h][1]: dst}))

    def z_copy(dst, src):
        return remote(zs.at[dst], rz.at[src], s_z.at[dst], r_z, me.at(z=dst))

    def az_copy(dst, src):
        return remote(agz.at[src], agz.at[src], s_az, r_az.at[src], me.at(z=dst))

    def copy_d(h, dst, src):
        part = dback.at[h, src]
        return remote(part, part, s_d.at[h], r_d.at[h], me.at(**{axes[h][1]: dst}))

    def copy_f(h, dst, src):
        part = fback.at[h, src]
        return remote(part, part, s_f.at[h], r_f.at[h, src], me.at(**{axes[h][0]: dst}))

    def copy_g(h, j):
        return remote(fback.at[h, j], gback.at[h, j], s_g.at[h], r_g.at[h], other_core)

    def entity_block(x):
        lanes = pl.ds(pl.multiple_of(x * NDOM, NDOM), NDOM)
        es[x, :, 0:NDOM] = nt(dh[...], h1[lanes, :]).astype(BF16)
        es[x, :, NDOM : 2 * NDOM] = nt(ql[...], av[lanes, :]).astype(BF16)

    def entity_out(x):
        for p in range(NB):
            ent_copy(p, x, me.x).start()

    def relation_block(c, y):
        lanes = pl.ds(pl.multiple_of((c * NY + y) * WIDE, WIDE), WIDE)
        return nn(dr[...], r1[:, lanes])

    def to_core(j):
        oc[j] = relation_block(1 - me.c, j).astype(BF16)
        core_copy(j).start()

    def with_core(j):
        block = relation_block(me.c, j)
        core_copy(j).wait_recv()
        block = (block + rc[j].astype(F32)).astype(BF16)
        for h in range(NH):
            asend[h, j] = block[:, h * LANES : (h + 1) * LANES]

            @pl.when(j != index[axes[h][0]])
            def _(h=h):
                copy_a(h, j, index[axes[h][0]]).start()

    def each(body):
        def step(k, carry):
            body(lax.rem(me.y + k, NY))
            return carry

        lax.fori_loop(1, NY + 1, step, 0)

    def four(ref, h):
        return sum(ref[h, j].astype(F32) for j in range(NY))

    def rel_second(h):
        first, second = axes[h]
        aland[h, index[first]] = asend[h, index[first]]
        arrived(aland.at[h, pl.ds(0, NY - 1)], r_a.at[h])
        total = four(aland, h).astype(BF16)
        for j in range(NX):
            n = min(XROWS, D - j * XROWS)
            bsend[h, j, 0:n] = total[j * XROWS : j * XROWS + n]
            if n < XROWS:
                bsend[h, j, n:] = jnp.zeros((XROWS - n, LANES), BF16)
        me.others(second, lambda q: copy_b(h, q, index[second]).start())

    def tiles(body, parts=range(NH)):
        def step(i, carry):
            z = lax.div(i, XTILES) * 8 + lax.rem(i, XTILES)

            @pl.when(z != me.z)
            def _():
                body(z)

            return carry

        lax.fori_loop(parts[0] * XTILES, (parts[-1] + 1) * XTILES, step, 0)

    def rel_z(h):
        second = axes[h][1]
        bland[h, index[second]] = bsend[h, index[second]]
        arrived(bland.at[h, pl.ds(0, NX - 1)], r_b.at[h])
        zs[h * 8 : h * 8 + XTILES] = four(bland, h).astype(BF16).reshape(XTILES, 16, LANES)
        def to_owner(q):
            @pl.when(jnp.logical_and(lax.div(q, 8) == h, lax.rem(q, 8) < XTILES))
            def _():
                z_copy(q, me.z).start()

        me.others("z", to_owner)

    owns = lax.rem(me.z, 8) < XTILES

    def rel_az():
        @pl.when(owns)
        def _():
            rz[me.z] = zs[me.z]
            arrived(rz.at[pl.ds(0, NZ - 1)], r_z)
            total = rz[0].astype(F32)
            for z in range(1, NZ):
                total += rz[z].astype(F32)
            agz[me.z] = total.astype(BF16)
            me.others("z", lambda q: az_copy(q, me.z).start())

    def rel_back1(h):
        second = axes[h][1]
        tiles(lambda q: az_copy(q, q).wait_recv(), (h,))
        dback[h, index[second]] = agz[h * 8 : h * 8 + XTILES].reshape(XROWS, LANES)
        me.others(second, lambda q: copy_d(h, q, index[second]).start())

    def rel_back2(h):
        first = axes[h][0]
        arrived(dback.at[h, pl.ds(0, NX - 1)], r_d.at[h])
        for j in range(NX):
            n = min(XROWS, D - j * XROWS)
            fback[h, index[first], j * XROWS : j * XROWS + n] = dback[h, j, 0:n]
        me.others(first, lambda q: copy_f(h, q, index[first]).start())
        copy_g(h, index[first]).start()

    def rel_core():
        def step(k, carry):
            for h in range(NH):
                j = lax.rem(index[axes[h][0]] + k, NX)
                copy_f(h, j, j).wait_recv()
                copy_g(h, j).start()
            return carry

        lax.fori_loop(1, NX, step, 0)

    def rel_done():
        low = me.c == 0
        for h in range(NH):
            arrived(gback.at[h], r_g.at[h])
            for j in range(NY):
                here, there = fback[h, j].astype(F32), gback[h, j].astype(F32)
                for c in range(NC):
                    start = ((c * NY + j) * NH + h) * LANES
                    n = min(LANES, RELS - start)
                    block = jnp.where(low, here, there) if c == 0 else jnp.where(low, there, here)
                    rel_out[:, start : start + n] = block.astype(BF16)[:, 0:n]

    def ent_yc(p):
        d, n = BACK[p]
        rex[me.x, d : d + n] = es[me.x, d : d + n]
        arrived(rex.at[pl.ds(0, NX - 1), pl.ds(d, n)], r_e.at[p])
        total = sum(rex[x, d : d + n].astype(F32) for x in range(NX)).astype(BF16)
        turned = nt(by_owner(), total).astype(BF16).reshape(NYC, 2 * NZ, n)
        sb1[p][...] = turned
        me.others("yc", lambda q: b1_copy(p, q, me.yc).start())
        rb1[p][me.yc] = sb1[p][me.yc]

    def ent_rows(p):
        arrived(rb1[p].at[pl.ds(0, NYC - 1)], r_b1.at[p])
        turned = tn(swap_zy(), rb1[p][...].reshape(2 * NDOM, BACK[p][1])).astype(BF16)
        sb2[p][...] = turned.reshape(NZ, 2 * NYC, BACK[p][1])
        rb2[p][me.z] = sb2[p][me.z]

    def ent_z(p):
        me.others("z", lambda q: b2_copy(p, q, me.z).start())

    def ent_done(p, pick):
        d, n = BACK[p]
        arrived(rb2[p].at[pl.ds(0, NZ - 1)], r_b2.at[p])
        ent_out[d : d + n, :] = tn(rb2[p][...].reshape(2 * NDOM, n), pick).astype(BF16)
    each(to_core)
    each(with_core)
    me.others("x", entity_block)
    entity_block(me.x)
    parts = jnp.concatenate([onehot(iota(sq, 0) == plan[h : h + 1, :]) for h in range(2)], axis=1)
    pick = nt(by_send_order(), parts).astype(BF16)
    rel_second(0)
    me.others("x", entity_out)
    rel_second(1)
    for h in range(NH):
        rel_z(h)
    for p in range(NB):
        ent_yc(p)
    rel_az()
    for p in range(NB):
        ent_rows(p)
    for h in range(NH):
        rel_back1(h)
    for p in range(NB):
        ent_z(p)
    for h in range(NH):
        rel_back2(h)
    rel_core()
    rel_done()
    for p in range(NB):
        ent_done(p, pick)
    arrived(gx.at[pl.ds(0, NX - 1)], s_3)
    arrived(es.at[pl.ds(0, NX - 1)], s_e)
    for p in range(NP):
        arrived(snd1[p].at[pl.ds(0, NZ - 1)], s_1.at[p])
        arrived(snd2[p].at[pl.ds(0, NYC - 1)], s_2.at[p])
    for p in range(NB):
        arrived(sb1[p].at[pl.ds(0, NYC - 1)], s_b1.at[p])
        arrived(sb2[p].at[pl.ds(0, NZ - 1)], s_b2.at[p])
    arrived(oc, s_c)
    for h in range(NH):
        arrived(asend.at[h, pl.ds(0, NY - 1)], s_a.at[h])
        arrived(bsend.at[h, pl.ds(0, NX - 1)], s_b.at[h])
        arrived(dback.at[h, pl.ds(0, NX - 1)], s_d.at[h])
        arrived(fback.at[h, pl.ds(0, NY - 1)], s_f.at[h])
        arrived(gback.at[h], s_g.at[h])
    tiles(lambda q: z_copy(q, me.z).wait_send())

    @pl.when(owns)
    def _():
        arrived(agz.at[pl.ds(0, NZ - 1)], s_az)


def scratch():
    def bf16(*shape):
        return pltpu.VMEM(shape, BF16)

    dma = pltpu.SemaphoreType.DMA

    def rows(pieces, *lead):
        return tuple(bf16(*lead, n) for _, n in pieces)

    by_z, by_yc = rows(PIECES, NZ, 2 * NYC), rows(PIECES, NYC, 2 * NZ)
    back_z, back_yc = rows(BACK, NZ, 2 * NYC), rows(BACK, NYC, 2 * NZ)
    block, slots, tile = bf16(NX, D, WIDE), bf16(D, SLOTS), bf16(NZ, 16, LANES)
    half, thin = bf16(NH, NY, D, LANES), bf16(NH, NX, XROWS, LANES)
    hops = [dma((NP,)), dma((NP,))]
    sides = [dma((NH,)), dma((NH,))]
    return (
        [bf16(D, NDOM), bf16(D, RELS), pltpu.VMEM((2, NDOM), I32)]
        + [pltpu.VMEM((4, 1, SPAN), I32), pltpu.VMEM((8, SLOTS), I32)]
        + [by_z, by_z, by_yc, by_yc, block]
        + [bf16(D, ROWS), bf16(D, ROWS), bf16(ROWS, D), pltpu.VMEM((ROWS, 1), F32)]
        + [bf16(ROWS, SLOTS), bf16(ROWS, SLOTS), bf16(SLOTS, RELPAD)]
        + [slots, slots, slots, slots, slots, bf16(ROWS, SLOTS), slots]
        + [block, block, back_yc, back_yc, back_z, back_z]
        + [block, block, half, half, thin, thin, tile, tile, tile, thin, half, half]
        + [dma((7,))]
        + hops * 2
        + [dma, dma((NP,)), dma, dma((NB,))]
        + [dma((NB,))] * 4
        + [dma, dma((NY,))]
        + sides * 2
        + [dma((NZ,)), dma, dma, dma((NZ,))]
        + sides
        + [dma((NH,)), dma((NH, NY))]
        + sides
    )


def per_device(entity, relation, head_ids, relation_ids, tail_ids, negative_ids, span_counts, plan):
    ent_out, rel_out = pl.pallas_call(
        kernel,
        out_shape=(
            jax.ShapeDtypeStruct((D, NDOM), BF16),
            jax.ShapeDtypeStruct((D, RELS), BF16),
        ),
        in_specs=[pl.BlockSpec(memory_space=pltpu.SMEM)] + [HBM] * 7,
        out_specs=(VMEM, VMEM),
        scratch_shapes=scratch(),
        compiler_params=pltpu.CompilerParams(
            collective_id=0, has_side_effects=True, vmem_limit_bytes=40 << 20
        ),
        name="bucket_round",
    )(
        span_counts,
        *(
            pltpu.with_memory_space_constraint(v, pltpu.HBM)
            for v in (
                jnp.transpose(entity, (1, 2, 0)),
                relation.T,
                head_ids.reshape(1, SPAN),
                relation_ids.reshape(1, SPAN),
                tail_ids.reshape(1, SPAN),
                negative_ids,
                plan.T,
            )
        ),
    )
    return jnp.transpose(ent_out.reshape(1, D, NDOM), (2, 0, 1)), rel_out.T


def solution(mesh):
    placed = (
        P(None, "dom", None),
        P(),
        P(("dom", "rep")),
        P(("dom", "rep")),
        P(("dom", "rep")),
        P(("dom", "rep"), None),
        P(("dom", "rep")),
        P(),
    )
    return jax.shard_map(
        per_device,
        mesh=mesh,
        in_specs=placed,
        out_specs=(P(None, ("dom", "rep"), None), P()),
        check_vma=False,
    )
```
